256 devices in a mesh: blk: 64 (over z, y, x_lo), off: 4 (over x_hi, core).
Axes of the slice: x: 4 (x_hi: 2, x_lo: 2; x = x_hi * 2 + x_lo), y: 4, z: 8, core: 2. Of those that a mesh axis runs over, the one named last changes fastest.
Arguments:
- traces: bfloat16 [64, 4, 1024, 2048], P('blk', 'off'), may hold values from -6 to 6
- tables: bfloat16 [64, 128, 2, 2048], P('blk'), may hold values from 0 to 7, as said below
- band_start: int32 [64, 4, 5, 1024], P('blk', 'off'), may hold values from 0 to 2032
- src_station: int32 [64], replicated, may hold values from 0 to 127
- rec_station: int32 [64, 4, 1024], P(None, 'off'), may hold values from 0 to 127
- aperture: int32 [64, 5], replicated, may hold values from 0 to 63, as said below
- aperture_weight: float32 [64, 5], replicated, may hold values from 0.5 to 1.5
Outputs:
- image_out: float32 [64, 2048], P('blk')
The draws below stay inside these ranges and needn't reach their ends.
Inputs may be any that keep to these rules, and one draw needn't show every extreme that they name: `aperture`: each row b lists 5 distinct tile ids: b itself, (b - 3) and (b + 3) modulo 64, and others within 3 positions of b around the closed cycle of 64 tiles, in any order. `tables`: index 0 holds traveltimes from 0 to 7 samples, index 1 amplitudes from 0.25 to 2.
All inputs are finite; a program needn't handle non-finite values.
Results may differ from the reference program's by a relative error of at most 0.0003.
Values may be sent and summed in bfloat16 or wider, within the bound.
A program may use at most 128 MiB of HBM per device.

```python
import math
import jax
import jax.numpy as jnp
from jax import lax

P_SIZE = 2048
TR = 1024
NT = 2048
NSTA = 128
BW = 16
APER = 5
HALF = 3
TILES = 64
GROUPS = 4


def draw_tables(key, part):
    first_key = jax.random.fold_in(key, 11)
    second_key = jax.random.fold_in(key, 12)
    times = jax.random.uniform(first_key, (TILES, NSTA, 1, P_SIZE), jnp.float32, 0.0, 0.5 * (BW - 2))
    amplitudes = jnp.exp(jax.random.uniform(second_key, (TILES, NSTA, 1, P_SIZE), jnp.float32, math.log(0.25), math.log(2.0)))
    return jnp.concatenate([times, amplitudes], axis=2).astype(jnp.bfloat16)


def draw_aperture(key, part):
    inner_offsets = jnp.concatenate([jnp.arange(-(HALF - 1), 0, dtype=jnp.int32), jnp.arange(1, HALF, dtype=jnp.int32)])
    fixed_offsets = jnp.array([-HALF, 0, HALF], dtype=jnp.int32)

    def draw_row(tile_index):
        first_key = jax.random.fold_in(jax.random.fold_in(key, 31), tile_index)
        second_key = jax.random.fold_in(first_key, 7919)
        picked = jax.random.permutation(first_key, inner_offsets)[:APER - 3]
        offsets = jnp.concatenate([fixed_offsets, picked])
        offsets = jax.random.permutation(second_key, offsets)
        return (tile_index + offsets) % TILES
    return jax.vmap(draw_row)(jnp.arange(TILES, dtype=jnp.int32)).astype(jnp.int32)


def set_ends(entries, own_key, low, largest):
    longest = entries.shape.index(max(entries.shape))
    spots = []
    for shift in (0, 1):
        where = [jax.random.randint(jax.random.fold_in(own_key, axis), (), 0, length) for axis, length in enumerate(entries.shape)]
        where[longest] = (where[longest] + shift) % entries.shape[longest]
        spots.append(tuple(where))
    return entries.at[spots[0]].set(low).at[spots[1]].set(largest)


def steps_of(key, dims, split, low, high):
    def one(axis_at, shards_of):
        steps = jax.random.uniform(jax.random.fold_in(jax.random.fold_in(key, 6), axis_at), (shards_of,), jnp.float32, low / len(split), high / len(split))
        return jnp.repeat(jnp.exp(steps), dims[axis_at] // shards_of).reshape((-1,) + (1,) * (len(dims) - axis_at - 1))

    factor_of = one(*split[0])
    for cut in split[1:]:
        factor_of = factor_of * one(*cut)
    return factor_of


def normal_values(key, shape, scale, bound, pieces=(), kind=jnp.bfloat16):
    factor_of = steps_of(key, shape, pieces, -0.22, 0.18) if pieces else 1.0
    result = jax.random.normal(key, shape, jnp.float32) * scale * factor_of
    return jnp.minimum(jnp.maximum(result, -bound), bound).astype(kind)


def setup_inputs(seed: int = 0) -> dict:
    keys = jax.random.split(jax.random.key(seed), 8)
    return {
        "traces": normal_values(keys[0], (TILES, GROUPS, TR, NT), 1.0, 6.0, ((0, 64), (1, 4))),
        "tables": draw_tables(jax.random.fold_in(keys[7], 71), 0),
        "band_start": set_ends(jax.random.randint(keys[2], (TILES, GROUPS, APER, TR), 0, NT - BW + 1), jax.random.fold_in(keys[2], 1), 0, NT - BW).astype(jnp.int32),
        "src_station": set_ends(jax.random.randint(keys[3], (TILES,), 0, NSTA), jax.random.fold_in(keys[3], 1), 0, NSTA - 1).astype(jnp.int32),
        "rec_station": set_ends(jax.random.randint(keys[4], (TILES, GROUPS, TR), 0, NSTA), jax.random.fold_in(keys[4], 1), 0, NSTA - 1).astype(jnp.int32),
        "aperture": draw_aperture(jax.random.fold_in(keys[7], 71), 0),
        "aperture_weight": jnp.clip(jax.random.uniform(keys[6], (TILES, APER), jnp.float32, 0.5, 1.5), 0.5, 1.5),
    }


def reference(traces, tables, band_start, src_station, rec_station, aperture, aperture_weight):
    norm_scale = 1.0 / math.sqrt(TR * GROUPS * APER)
    tap_range = jnp.arange(BW, dtype=jnp.int32)

    def pair_term(pair_index):
        block_id = (pair_index // APER).astype(jnp.int32)
        slot_number = (pair_index % APER).astype(jnp.int32)
        target = aperture[block_id, slot_number].astype(jnp.int32)
        tile_table = lax.dynamic_index_in_dim(tables, target, 0, keepdims=False).astype(jnp.float32)
        source_vals = tile_table[src_station[block_id]]
        receiver_vals = tile_table[rec_station[block_id]]
        arrival = source_vals[0][None, None, :] + receiver_vals[:, :, 0, :]
        weight = source_vals[1][None, None, :] * receiver_vals[:, :, 1, :]
        trace_rows = lax.dynamic_index_in_dim(traces, block_id, 0, keepdims=False)
        block_starts = lax.dynamic_index_in_dim(band_start, block_id, 0, keepdims=False)
        starts = jnp.take(block_starts, slot_number, axis=1)
        sample_index = (starts[:, :, None] + tap_range[None, None, :]).astype(jnp.int32)
        trace_band = jnp.take_along_axis(trace_rows, sample_index, axis=2).astype(jnp.float32)
        interp = jnp.zeros(arrival.shape, jnp.float32)
        for tap_number in range(BW):
            interp = interp + jnp.maximum(0.0, 1.0 - jnp.abs(arrival - tap_number)) * trace_band[:, :, tap_number][:, :, None]
        return aperture_weight[block_id, slot_number] * lax.optimization_barrier(jnp.sum(weight * interp, axis=(0, 1)))
    all_terms = lax.map(pair_term, jnp.arange(TILES * APER, dtype=jnp.int32))
    image_sum = jnp.zeros((TILES, P_SIZE), jnp.float32).at[aperture.reshape(-1)].add(all_terms)
    return image_sum * norm_scale
```

```python
import functools
import math

import jax
import jax.numpy as jnp
from jax import lax
from jax.experimental import pallas as pl
from jax.experimental.pallas import tpu as pltpu
from jax.sharding import PartitionSpec as P

BW = 16
APER = 5
HALF = 3
NOFF = 2 * HALF + 1
LANES = 128
CHUNKS = 8
STEP = 16
MESH = pl.DeviceIdType.MESH


def lane_take(x, idx):
    return jnp.take_along_axis(x, idx, axis=1, mode="promise_in_bounds")


def kernel(
    tiles, groups, scale,
    traces, tabs, starts, src, rec, aper, aw,
    out,
    trace_v, tabs_v, tab32, starts_v, src_v, rec_v, aper_v, aw_v,
    pos_v, window_v, send_v, recv_v, low_v, slope_v, source_v,
    load_sem, chunk_sem, send_sem, recv_sem, peer_send_sem, peer_recv_sem,
):
    rows, samples = trace_v.shape
    stations = send_v.shape[1]
    blk = lax.axis_index("blk")
    off = lax.axis_index("off")

    def at_tile(d):
        return lax.rem(blk + (d + tiles), tiles)

    barrier = pltpu.get_barrier_semaphore()
    for step in range(1, groups):
        pl.semaphore_signal(
            barrier, inc=1, device_id=(blk, lax.rem(off + step, groups)), device_id_type=MESH
        )

    @pl.when(off > 0)
    def _():
        for sign in (-1, 1):
            for g in range(groups):
                other = lax.rem(blk + sign * off + tiles, tiles)
                pl.semaphore_signal(barrier, inc=1, device_id=(other, g), device_id_type=MESH)

    small = [
        pltpu.make_async_copy(starts, starts_v, load_sem.at[0]),
        pltpu.make_async_copy(aper, aper_v, load_sem.at[1]),
        pltpu.make_async_copy(rec.at[blk], rec_v, load_sem.at[2]),
        pltpu.make_async_copy(aw, aw_v, load_sem.at[3]),
        pltpu.make_async_copy(src, src_v, load_sem.at[4]),
    ]
    for copy in small:
        copy.start()
    per = rows // CHUNKS

    def chunk_copy(i):
        span = pl.ds(pl.multiple_of(i * per, per), per)
        return pltpu.make_async_copy(traces.at[span], trace_v.at[span], chunk_sem.at[i])

    for i in range(CHUNKS):
        chunk_copy(i).start()
    tabs_copy = pltpu.make_async_copy(tabs, tabs_v, load_sem.at[5])
    tabs_copy.start()

    small[0].wait()
    small[1].wait()
    small[3].wait()
    mine = lax.broadcasted_iota(jnp.int32, (APER, tiles), 1) == blk
    target = jnp.sum(jnp.where(mine, aper_v[...], 0), axis=1, keepdims=True)
    taper = jnp.sum(jnp.where(mine, aw_v[...], 0.0), axis=1, keepdims=True)
    place = lax.rem(target - blk + (HALF + tiles), tiles)
    lane_off = lax.broadcasted_iota(jnp.int32, (APER, LANES), 1) // BW
    hit = (lane_off == place).astype(jnp.float32)
    taper_row = jnp.sum(hit * taper, axis=0, keepdims=True)
    begin = starts_v[:, 0, :]
    high = (begin >> 7).astype(jnp.float32)
    low = (begin & (LANES - 1)).astype(jnp.float32)
    fill = jnp.zeros((8 - APER, rows), jnp.float32)
    digits = jnp.concatenate([high, fill, low, fill], axis=0).astype(jnp.bfloat16)
    gap = jnp.zeros((8 - APER, LANES), jnp.float32)
    pick = jnp.concatenate([hit * LANES, gap, hit, gap], axis=0).astype(jnp.bfloat16)
    first = lax.dot_general(
        digits, pick, (((0,), (0,)), ((), ())), preferred_element_type=jnp.float32
    )
    tap = lax.broadcasted_iota(jnp.int32, (rows, LANES), 1) & (BW - 1)
    pos_v[...] = first.astype(jnp.int32) + tap

    def do_chunk(i, carry):
        chunk_copy(i).wait()

        def do_rows(k, inner):
            span = pl.ds(pl.multiple_of(i * per + k * STEP, STEP), STEP)
            pos = pos_v[span, :]
            inside = pos & (LANES - 1)
            block = pos >> 7
            acc = jnp.zeros((STEP, LANES), jnp.float32)
            for c in range(samples // LANES):
                piece = trace_v[span, c * LANES:(c + 1) * LANES].astype(jnp.float32)
                acc = jnp.where(block == c, lane_take(piece, inside), acc)
            window_v[span, :] = acc.astype(jnp.bfloat16)
            return inner

        return lax.fori_loop(0, per // STEP, do_rows, carry)

    lax.fori_loop(0, CHUNKS, do_chunk, 0)

    small[2].wait()
    onehot = (
        lax.broadcasted_iota(jnp.int32, (stations, rows), 0) == rec_v[...]
    ).astype(jnp.float32).astype(jnp.bfloat16)
    sums = jnp.dot(onehot, window_v[...], preferred_element_type=jnp.float32) * taper_row
    send_v[...] = sums.T

    pl.semaphore_wait(barrier, groups - 1 + 2 * HALF)

    def band_copy(d):
        slot = 1 if d > 0 else 0
        o = d + HALF
        return pltpu.make_async_remote_copy(
            src_ref=send_v.at[pl.ds(o * BW, BW)],
            dst_ref=recv_v.at[slot, off],
            send_sem=send_sem.at[o],
            recv_sem=recv_sem.at[slot, off],
            device_id=(at_tile(d), abs(d)),
            device_id_type=MESH,
        )

    def band_wait(slot, g):
        pltpu.make_async_remote_copy(
            src_ref=send_v.at[pl.ds(0, BW)],
            dst_ref=recv_v.at[slot, g],
            send_sem=send_sem.at[0],
            recv_sem=recv_sem.at[slot, g],
            device_id=(blk, off),
            device_id_type=MESH,
        ).wait_recv()

    for d in (-3, 3, -2, 2, -1, 1):
        band_copy(d).start()

    @pl.when(off > 0)
    def _():
        band_copy(0).start()

    @pl.when(off == 0)
    def _():
        recv_v[0, 0] = send_v[HALF * BW:(HALF + 1) * BW, :]
        recv_v[1] = jnp.zeros(recv_v.shape[1:], jnp.float32)

    tabs_copy.wait()
    small[4].wait()
    cols = tab32.shape[0] // stations // 2
    origins = (at_tile(off), lax.rem(blk - off + tiles, tiles))
    lane = lax.broadcasted_iota(jnp.int32, (1, tiles), 1)
    source_ids = [
        jnp.sum(jnp.where(lane == origin, src_v[...], 0), axis=1, keepdims=True)
        for origin in origins
    ]

    def widen(r, rows_of):
        span = pl.ds(pl.multiple_of(r * (2 * cols), 2 * cols), 2 * cols)
        wide = tabs_v[span, :].astype(jnp.float32)
        tab32[span, :] = wide
        return tuple(jnp.where(i == r, wide, old) for i, old in zip(source_ids, rows_of))

    blank = jnp.zeros((2 * cols, LANES), jnp.float32)
    found = lax.fori_loop(0, stations, widen, (blank, blank), unroll=4)
    source_v[0] = found[0]
    source_v[1] = found[1]

    for g in range(groups):
        if g == 0:
            @pl.when(off > 0)
            def _():
                band_wait(0, 0)
        else:
            band_wait(0, g)

    @pl.when(off > 0)
    def _():
        for g in range(groups):
            band_wait(1, g)

    base = []
    slope = []
    tap_id = lax.broadcasted_iota(jnp.int32, (BW, stations), 0).astype(jnp.float32)
    for slot in range(2):
        total = (recv_v[slot, 0] + recv_v[slot, 1]) + (recv_v[slot, 2] + recv_v[slot, 3])
        after = jnp.concatenate([total[1:], total[BW - 1:]], axis=0)
        step = after - total
        base.append(total - tap_id * step)
        slope.append(step)
    rest = jnp.zeros((LANES - 2 * BW, stations), jnp.float32)
    low_v[...] = jnp.concatenate(base + [rest], axis=0).T
    slope_v[...] = jnp.concatenate(slope + [rest], axis=0).T

    sources = [
        (source_v[slot, pl.ds(0, cols, stride=2), :], source_v[slot, pl.ds(1, cols, stride=2), :])
        for slot in range(2)
    ]

    def do_station(r, acc):
        row = pl.multiple_of(r * (2 * cols), 2 * cols)
        time = tab32[pl.ds(row, cols, stride=2), :]
        amp = tab32[pl.ds(row + 1, cols, stride=2), :]
        base_row = jnp.broadcast_to(low_v[pl.ds(r, 1), :], (cols, LANES))
        slope_row = jnp.broadcast_to(slope_v[pl.ds(r, 1), :], (cols, LANES))
        result = []
        for slot in range(2):
            arrival = sources[slot][0] + time
            cell = arrival.astype(jnp.int32) + BW * slot
            value = lane_take(base_row, cell) + lane_take(slope_row, cell) * arrival
            result.append(acc[slot] + amp * value)
        return tuple(result)

    zero = jnp.zeros((cols, LANES), jnp.float32)
    acc = lax.fori_loop(0, stations, do_station, (zero, zero), unroll=4)
    out[off] = (sources[0][1] * acc[0] + sources[1][1] * acc[1]) * scale

    def peer_copy(step):
        return pltpu.make_async_remote_copy(
            src_ref=out.at[off],
            dst_ref=out.at[off],
            send_sem=peer_send_sem.at[step - 1],
            recv_sem=peer_recv_sem.at[off],
            device_id=(blk, lax.rem(off + step, groups)),
            device_id_type=MESH,
        )

    for step in range(1, groups):
        peer_copy(step).start()
    for step in range(1, groups):
        other = lax.rem(off + step, groups)
        pltpu.make_async_remote_copy(
            src_ref=out.at[off],
            dst_ref=out.at[other],
            send_sem=peer_send_sem.at[step - 1],
            recv_sem=peer_recv_sem.at[other],
            device_id=(blk, other),
            device_id_type=MESH,
        ).wait_recv()
    for d in (-3, 3, -2, 2, -1, 1):
        band_copy(d).wait_send()

    @pl.when(off > 0)
    def _():
        band_copy(0).wait_send()

    for step in range(1, groups):
        peer_copy(step).wait_send()


def shards(traces, tables, band_start, src_vtation, rec_station, aperture, aperture_weight):
    tiles = lax.axis_size("blk")
    groups = lax.axis_size("off")
    rows, samples = traces.shape[2:]
    stations, _, points = tables.shape[1:]
    cols = points // LANES
    tabs = tables.reshape(stations, 2, cols, LANES).transpose(0, 2, 1, 3)
    tabs = tabs.reshape(stations * cols * 2, LANES)
    scale = 1.0 / math.sqrt(rows * groups * APER)
    any_spec = pl.BlockSpec(memory_space=pltpu.HBM)
    parts = pl.pallas_call(
        functools.partial(kernel, tiles, groups, scale),
        out_shape=jax.ShapeDtypeStruct((groups, cols, LANES), jnp.float32),
        in_specs=[any_spec] * 7,
        out_specs=pl.BlockSpec(memory_space=pltpu.VMEM),
        scratch_shapes=[
            pltpu.VMEM((rows, samples), jnp.bfloat16),
            pltpu.VMEM(tabs.shape, jnp.bfloat16),
            pltpu.VMEM(tabs.shape, jnp.float32),
            pltpu.VMEM((APER, 1, rows), jnp.int32),
            pltpu.VMEM((1, tiles), jnp.int32),
            pltpu.VMEM((1, rows), jnp.int32),
            pltpu.VMEM((APER, tiles), jnp.int32),
            pltpu.VMEM((APER, tiles), jnp.float32),
            pltpu.VMEM((rows, LANES), jnp.int32),
            pltpu.VMEM((rows, LANES), jnp.bfloat16),
            pltpu.VMEM((LANES, stations), jnp.float32),
            pltpu.VMEM((2, groups, BW, stations), jnp.float32),
            pltpu.VMEM((stations, LANES), jnp.float32),
            pltpu.VMEM((stations, LANES), jnp.float32),
            pltpu.VMEM((2, 2 * cols, LANES), jnp.float32),
            pltpu.SemaphoreType.DMA((6,)),
            pltpu.SemaphoreType.DMA((CHUNKS,)),
            pltpu.SemaphoreType.DMA((NOFF,)),
            pltpu.SemaphoreType.DMA((2, groups)),
            pltpu.SemaphoreType.DMA((groups - 1,)),
            pltpu.SemaphoreType.DMA((groups,)),
        ],
        compiler_params=pltpu.CompilerParams(
            collective_id=0, has_side_effects=True, vmem_limit_bytes=60 * 1024 * 1024
        ),
        name="migrate",
    )(
        traces.reshape(rows, samples),
        tabs,
        band_start.reshape(APER, 1, rows),
        src_vtation.reshape(1, tiles),
        rec_station,
        aperture.T,
        aperture_weight.T,
    )
    return jnp.sum(parts, axis=0).reshape(1, points)


def solution(mesh):
    placed = (
        P("blk", "off", None, None),
        P("blk", None, None, None),
        P("blk", "off", None, None),
        P(),
        P(None, "off", None),
        P(),
        P(),
    )
    return jax.shard_map(
        shards, mesh=mesh, in_specs=placed, out_specs=P("blk", None), check_vma=False
    )
```

```python
import functools
import math

import jax
import jax.numpy as jnp
from jax import lax
from jax.experimental import pallas as pl
from jax.experimental.pallas import tpu as pltpu
from jax.sharding import PartitionSpec as P

BW = 16
APER = 5
HALF = 3
NOFF = 2 * HALF + 1
LANES = 128
CHUNKS = 4
STEP = 16
UNROLL = 16
MESH = pl.DeviceIdType.MESH


def lane_take(x, idx):
    numbers = lax.GatherDimensionNumbers(
        offset_dims=(),
        collapsed_slice_dims=(1,),
        start_index_map=(1,),
        operand_batching_dims=(0,),
        start_indices_batching_dims=(0,),
    )
    return lax.gather(
        x, idx[..., None], numbers, slice_sizes=(1, 1),
        mode=lax.GatherScatterMode.PROMISE_IN_BOUNDS,
    )


def kernel(
    tiles, groups, scale,
    traces, tabs, starts, src, rec, aper, aw,
    out,
    trace_v, tabs_v, tab32, starts_v, src_v, rec_v, aper_v, aw_v,
    pos_v, window_v, send_v, recv_v, table_v, source_v,
    load_sem, chunk_sem, send_sem, recv_sem, peer_send_sem, peer_recv_sem,
):
    rows, samples = trace_v.shape
    stations = send_v.shape[1]
    blk = lax.axis_index("blk")
    off = lax.axis_index("off")

    def at_tile(d):
        return lax.rem(blk + (d + tiles), tiles)

    barrier = pltpu.get_barrier_semaphore()
    for step in range(1, groups):
        pl.semaphore_signal(
            barrier, inc=1, device_id=(blk, lax.rem(off + step, groups)), device_id_type=MESH
        )

    @pl.when(off > 0)
    def _():
        for sign in (-1, 1):
            for g in range(groups):
                other = lax.rem(blk + sign * off + tiles, tiles)
                pl.semaphore_signal(barrier, inc=1, device_id=(other, g), device_id_type=MESH)

    small = [
        pltpu.make_async_copy(starts, starts_v, load_sem.at[0]),
        pltpu.make_async_copy(aper, aper_v, load_sem.at[1]),
        pltpu.make_async_copy(rec.at[blk], rec_v, load_sem.at[2]),
        pltpu.make_async_copy(aw, aw_v, load_sem.at[3]),
        pltpu.make_async_copy(src, src_v, load_sem.at[4]),
    ]
    for copy in small:
        copy.start()
    per = rows // CHUNKS

    def chunk_copy(i):
        span = pl.ds(pl.multiple_of(i * per, per), per)
        return pltpu.make_async_copy(traces.at[span], trace_v.at[span], chunk_sem.at[i])

    for i in range(CHUNKS):
        chunk_copy(i).start()
    tabs_copy = pltpu.make_async_copy(tabs, tabs_v, load_sem.at[5])
    tabs_copy.start()

    small[0].wait()
    small[1].wait()
    small[3].wait()
    mine = lax.broadcasted_iota(jnp.int32, (APER, tiles), 1) == blk
    target = jnp.sum(jnp.where(mine, aper_v[...], 0), axis=1, keepdims=True)
    taper = jnp.sum(jnp.where(mine, aw_v[...], 0.0), axis=1, keepdims=True)
    place = lax.rem(target - blk + (HALF + tiles), tiles)
    lane_off = lax.broadcasted_iota(jnp.int32, (APER, LANES), 1) // BW
    hit = (lane_off == place).astype(jnp.float32)
    taper_row = jnp.sum(hit * taper, axis=0, keepdims=True)
    begin = starts_v[:, 0, :]
    high = (begin >> 7).astype(jnp.float32)
    low = (begin & (LANES - 1)).astype(jnp.float32)
    fill = jnp.zeros((8 - APER, rows), jnp.float32)
    digits = jnp.concatenate([high, fill, low, fill], axis=0).astype(jnp.bfloat16)
    gap = jnp.zeros((8 - APER, LANES), jnp.float32)
    pick = jnp.concatenate([hit * LANES, gap, hit, gap], axis=0).astype(jnp.bfloat16)
    first = lax.dot_general(
        digits, pick, (((0,), (0,)), ((), ())), preferred_element_type=jnp.float32
    )
    tap = lax.broadcasted_iota(jnp.int32, (rows, LANES), 1) & (BW - 1)
    pos_v[...] = (first.astype(jnp.int32) + tap).astype(jnp.int16)

    small[2].wait()
    station_id = lax.broadcasted_iota(jnp.int32, (stations, per), 0)
    sums = jnp.zeros((stations, LANES), jnp.float32)
    for i in range(CHUNKS):
        chunk_copy(i).wait()

        def do_rows(k, inner, i=i):
            span = pl.ds(pl.multiple_of(i * per + k * STEP, STEP), STEP)
            pos = pos_v[span, :]
            inside = pos & jnp.int16(LANES - 1)
            block = pos >> jnp.int16(7)
            acc = jnp.zeros((STEP, LANES), jnp.bfloat16)
            for c in range(samples // LANES):
                piece = lane_take(trace_v[span, c * LANES:(c + 1) * LANES], inside)
                acc = jnp.where(block == jnp.int16(c), piece, acc)
            window_v[span, :] = acc
            return inner

        lax.fori_loop(0, per // STEP, do_rows, 0, unroll=min(UNROLL, per // STEP))
        onehot = (station_id == rec_v[:, i * per:(i + 1) * per]).astype(jnp.float32)
        sums = sums + jnp.dot(
            onehot.astype(jnp.bfloat16),
            window_v[i * per:(i + 1) * per, :],
            preferred_element_type=jnp.float32,
        )
    send_v[...] = (sums * taper_row).T

    pl.semaphore_wait(barrier, groups - 1 + 2 * HALF)

    def band_copy(d):
        slot = 1 if d > 0 else 0
        o = d + HALF
        return pltpu.make_async_remote_copy(
            src_ref=send_v.at[pl.ds(o * BW, BW)],
            dst_ref=recv_v.at[slot, off],
            send_sem=send_sem.at[o],
            recv_sem=recv_sem.at[slot, off],
            device_id=(at_tile(d), abs(d)),
            device_id_type=MESH,
        )

    def band_wait(slot, g):
        pltpu.make_async_remote_copy(
            src_ref=send_v.at[pl.ds(0, BW)],
            dst_ref=recv_v.at[slot, g],
            send_sem=send_sem.at[0],
            recv_sem=recv_sem.at[slot, g],
            device_id=(blk, off),
            device_id_type=MESH,
        ).wait_recv()

    for d in (-3, 3, -2, 2, -1, 1):
        band_copy(d).start()

    @pl.when(off > 0)
    def _():
        band_copy(0).start()

    @pl.when(off == 0)
    def _():
        recv_v[0, 0] = send_v[HALF * BW:(HALF + 1) * BW, :]
        recv_v[1] = jnp.zeros(recv_v.shape[1:], jnp.float32)

    tabs_copy.wait()
    small[4].wait()
    cols = tab32.shape[0] // stations // 2
    origins = (at_tile(off), lax.rem(blk - off + tiles, tiles))
    lane = lax.broadcasted_iota(jnp.int32, (1, tiles), 1)
    source_ids = [
        jnp.sum(jnp.where(lane == origin, src_v[...], 0), axis=1, keepdims=True)
        for origin in origins
    ]

    def widen(r, rows_of):
        span = pl.ds(pl.multiple_of(r * (2 * cols), 2 * cols), 2 * cols)
        wide = tabs_v[span, :].astype(jnp.float32)
        tab32[span, :] = wide
        return tuple(jnp.where(i == r, wide, old) for i, old in zip(source_ids, rows_of))

    blank = jnp.zeros((2 * cols, LANES), jnp.float32)
    found = lax.fori_loop(0, stations, widen, (blank, blank), unroll=4)
    source_v[0] = found[0]
    source_v[1] = found[1]

    for g in range(groups):
        if g == 0:
            @pl.when(off > 0)
            def _():
                band_wait(0, 0)
        else:
            band_wait(0, g)

    @pl.when(off > 0)
    def _():
        for g in range(groups):
            band_wait(1, g)

    base = []
    slope = []
    for slot in range(2):
        total = (recv_v[slot, 0] + recv_v[slot, 1]) + (recv_v[slot, 2] + recv_v[slot, 3])
        after = jnp.concatenate([total[1:], total[BW - 1:]], axis=0)
        base.append(total)
        slope.append(after - total)
    rest = jnp.zeros((LANES - 4 * BW, stations), jnp.float32)
    both = jnp.concatenate(base + slope + [rest], axis=0).T
    for n, table in enumerate((both, pltpu.roll(both, LANES - 2 * BW, 1))):
        upper = table.astype(jnp.bfloat16)
        table_v[2 * n] = upper
        table_v[2 * n + 1] = (table - upper.astype(jnp.float32)).astype(jnp.bfloat16)

    def do_column(c, carry):
        time_at = [source_v[slot, pl.ds(2 * c, 1), :] for slot in range(2)]
        amp_at = [source_v[slot, pl.ds(2 * c + 1, 1), :] for slot in range(2)]
        acc = [jnp.zeros((STEP, LANES), jnp.float32) for slot in range(2)]
        for first_station in range(0, stations, STEP):
            row = first_station * 2 * cols + 2 * c
            time = tab32[pl.ds(row, STEP, stride=2 * cols), :]
            amp = tab32[pl.ds(row + 1, STEP, stride=2 * cols), :]
            near = [table_v[n, first_station:first_station + STEP, :] for n in range(4)]
            for slot in range(2):
                arrival = time_at[slot] + time
                whole = arrival.astype(jnp.int32)
                part = arrival - whole.astype(jnp.float32)
                cell = whole.astype(jnp.int16)
                if slot:
                    cell = cell + jnp.int16(BW)
                got = [lane_take(x, cell).astype(jnp.float32) for x in near]
                value = (got[0] + got[1]) + (got[2] + got[3]) * part
                acc[slot] = acc[slot] + amp * value
        both_acc = amp_at[0] * acc[0] + amp_at[1] * acc[1]
        out[off, pl.ds(c, 1), :] = jnp.sum(both_acc, axis=0, keepdims=True) * scale
        return carry

    lax.fori_loop(0, cols, do_column, 0, unroll=2)

    def peer_copy(step):
        return pltpu.make_async_remote_copy(
            src_ref=out.at[off],
            dst_ref=out.at[off],
            send_sem=peer_send_sem.at[step - 1],
            recv_sem=peer_recv_sem.at[off],
            device_id=(blk, lax.rem(off + step, groups)),
            device_id_type=MESH,
        )

    for step in range(1, groups):
        peer_copy(step).start()
    for step in range(1, groups):
        other = lax.rem(off + step, groups)
        pltpu.make_async_remote_copy(
            src_ref=out.at[off],
            dst_ref=out.at[other],
            send_sem=peer_send_sem.at[step - 1],
            recv_sem=peer_recv_sem.at[other],
            device_id=(blk, other),
            device_id_type=MESH,
        ).wait_recv()
    for d in (-3, 3, -2, 2, -1, 1):
        band_copy(d).wait_send()

    @pl.when(off > 0)
    def _():
        band_copy(0).wait_send()

    for step in range(1, groups):
        peer_copy(step).wait_send()


def shards(traces, tables, band_start, src_vtation, rec_station, aperture, aperture_weight):
    tiles = lax.axis_size("blk")
    groups = lax.axis_size("off")
    rows, samples = traces.shape[2:]
    stations, _, points = tables.shape[1:]
    cols = points // LANES
    tabs = tables.reshape(stations, 2, cols, LANES).transpose(0, 2, 1, 3)
    tabs = tabs.reshape(stations * cols * 2, LANES)
    scale = 1.0 / math.sqrt(rows * groups * APER)
    any_spec = pl.BlockSpec(memory_space=pltpu.HBM)
    parts = pl.pallas_call(
        functools.partial(kernel, tiles, groups, scale),
        out_shape=jax.ShapeDtypeStruct((groups, cols, LANES), jnp.float32),
        in_specs=[any_spec] * 7,
        out_specs=pl.BlockSpec(memory_space=pltpu.VMEM),
        scratch_shapes=[
            pltpu.VMEM((rows, samples), jnp.bfloat16),
            pltpu.VMEM(tabs.shape, jnp.bfloat16),
            pltpu.VMEM(tabs.shape, jnp.float32),
            pltpu.VMEM((APER, 1, rows), jnp.int32),
            pltpu.VMEM((1, tiles), jnp.int32),
            pltpu.VMEM((1, rows), jnp.int32),
            pltpu.VMEM((APER, tiles), jnp.int32),
            pltpu.VMEM((APER, tiles), jnp.float32),
            pltpu.VMEM((rows, LANES), jnp.int16),
            pltpu.VMEM((rows, LANES), jnp.bfloat16),
            pltpu.VMEM((LANES, stations), jnp.float32),
            pltpu.VMEM((2, groups, BW, stations), jnp.float32),
            pltpu.VMEM((4, stations, LANES), jnp.bfloat16),
            pltpu.VMEM((2, 2 * cols, LANES), jnp.float32),
            pltpu.SemaphoreType.DMA((6,)),
            pltpu.SemaphoreType.DMA((CHUNKS,)),
            pltpu.SemaphoreType.DMA((NOFF,)),
            pltpu.SemaphoreType.DMA((2, groups)),
            pltpu.SemaphoreType.DMA((groups - 1,)),
            pltpu.SemaphoreType.DMA((groups,)),
        ],
        compiler_params=pltpu.CompilerParams(
            collective_id=0, has_side_effects=True, vmem_limit_bytes=60 * 1024 * 1024
        ),
        name="migrate",
    )(
        traces.reshape(rows, samples),
        tabs,
        band_start.reshape(APER, 1, rows),
        src_vtation.reshape(1, tiles),
        rec_station,
        aperture.T,
        aperture_weight.T,
    )
    return jnp.sum(parts, axis=0).reshape(1, points)


def solution(mesh):
    placed = (
        P("blk", "off", None, None),
        P("blk", None, None, None),
        P("blk", "off", None, None),
        P(),
        P(None, "off", None),
        P(),
        P(),
    )
    return jax.shard_map(
        shards, mesh=mesh, in_specs=placed, out_specs=P("blk", None), check_vma=False
    )
```

```python
import functools
import math

import jax
import jax.numpy as jnp
from jax import lax
from jax.experimental import pallas as pl
from jax.experimental.pallas import tpu as pltpu
from jax.sharding import PartitionSpec as P

BW = 16
APER = 5
HALF = 3
NOFF = 2 * HALF + 1
CORES = 2
SPLIT = 3
TAKEN = ((-2, -1, 1, SPLIT), (0, -3, 2, SPLIT))
SEND_ORDER = (3, 2, 1, 0, -1, -2, -3)
LANES = 128
CHUNKS = 4
STEP = 16
UNROLL = 16
MESH = pl.DeviceIdType.MESH


def lane_take(x, idx):
    numbers = lax.GatherDimensionNumbers(
        offset_dims=(),
        collapsed_slice_dims=(1,),
        start_index_map=(1,),
        operand_batching_dims=(0,),
        start_indices_batching_dims=(0,),
    )
    return lax.gather(
        x, idx[..., None], numbers, slice_sizes=(1, 1),
        mode=lax.GatherScatterMode.PROMISE_IN_BOUNDS,
    )


def kernel(
    tiles, groups, scale,
    traces, tabs, starts, src, rec, aper, aw,
    out,
    trace_v, tabs_v, tab32, starts_v, src_v, rec_v, aper_v, aw_v,
    pos_v, window_v, send_v, recv_v, table_v, source_v, time_v, amp_v, early_v,
    load_sem, chunk_sem, send_sem, recv_sem, peer_send_sem, peer_recv_sem,
):
    rows, samples = trace_v.shape
    stations = send_v.shape[1]
    blk = lax.axis_index("blk")
    off = lax.axis_index("off")

    def at_tile(d):
        return lax.rem(blk + (d + tiles), tiles)

    core = lax.rem(off, CORES)
    chip_first = off - core
    sibling = chip_first + (1 - core)

    def taken(slot):
        return jnp.where(core == 0, TAKEN[0][slot], TAKEN[1][slot])

    barrier = pltpu.get_barrier_semaphore()

    def greet(tile, g):
        pl.semaphore_signal(barrier, inc=1, device_id=(tile, g), device_id_type=MESH)

    for c in range(CORES):
        @pl.when(core == c)
        def _(c=c):
            for d in reversed(TAKEN[c]):
                if d:
                    for g in range(groups):
                        greet(at_tile(-d), g)
            if 0 in TAKEN[c]:
                for step in range(1, groups):
                    greet(blk, lax.rem(off + step, groups))
            else:
                greet(blk, sibling)

    small = [
        pltpu.make_async_copy(starts, starts_v, load_sem.at[0]),
        pltpu.make_async_copy(aper, aper_v, load_sem.at[1]),
        pltpu.make_async_copy(rec.at[blk], rec_v, load_sem.at[2]),
        pltpu.make_async_copy(aw, aw_v, load_sem.at[3]),
        pltpu.make_async_copy(src, src_v, load_sem.at[4]),
    ]
    for copy in small:
        copy.start()
    per = rows // CHUNKS

    def chunk_copy(i):
        span = pl.ds(pl.multiple_of(i * per, per), per)
        return pltpu.make_async_copy(traces.at[span], trace_v.at[span], chunk_sem.at[i])

    for i in range(CHUNKS):
        chunk_copy(i).start()
    tabs_copy = pltpu.make_async_copy(tabs, tabs_v, load_sem.at[5])
    tabs_copy.start()

    small[0].wait()
    small[1].wait()
    small[3].wait()
    mine = lax.broadcasted_iota(jnp.int32, (APER, tiles), 1) == blk
    target = jnp.sum(jnp.where(mine, aper_v[...], 0), axis=1, keepdims=True)
    taper = jnp.sum(jnp.where(mine, aw_v[...], 0.0), axis=1, keepdims=True)
    place = lax.rem(target - blk + (HALF + tiles), tiles)
    lane_off = lax.broadcasted_iota(jnp.int32, (APER, LANES), 1) // BW
    hit = (lane_off == place).astype(jnp.float32)
    taper_row = jnp.sum(hit * taper, axis=0, keepdims=True)
    begin = starts_v[:, 0, :]
    high = (begin >> 7).astype(jnp.float32)
    low = (begin & (LANES - 1)).astype(jnp.float32)
    fill = jnp.zeros((8 - APER, rows), jnp.float32)
    digits = jnp.concatenate([high, fill, low, fill], axis=0).astype(jnp.bfloat16)
    gap = jnp.zeros((8 - APER, LANES), jnp.float32)
    pick = jnp.concatenate([hit * LANES, gap, hit, gap], axis=0).astype(jnp.bfloat16)
    first = lax.dot_general(
        digits, pick, (((0,), (0,)), ((), ())), preferred_element_type=jnp.float32
    )
    tap = lax.broadcasted_iota(jnp.int32, (rows, LANES), 1) & (BW - 1)
    pos_v[...] = (first.astype(jnp.int32) + tap).astype(jnp.int16)

    small[2].wait()
    station_id = lax.broadcasted_iota(jnp.int32, (stations, per), 0)
    sums = jnp.zeros((stations, LANES), jnp.float32)
    for i in range(CHUNKS):
        chunk_copy(i).wait()

        def do_rows(k, inner, i=i):
            span = pl.ds(pl.multiple_of(i * per + k * STEP, STEP), STEP)
            pos = pos_v[span, :]
            inside = pos & jnp.int16(LANES - 1)
            block = pos >> jnp.int16(7)
            acc = jnp.zeros((STEP, LANES), jnp.bfloat16)
            for c in range(samples // LANES):
                piece = lane_take(trace_v[span, c * LANES:(c + 1) * LANES], inside)
                acc = jnp.where(block == jnp.int16(c), piece, acc)
            window_v[span, :] = acc
            return inner

        lax.fori_loop(0, per // STEP, do_rows, 0, unroll=min(UNROLL, per // STEP))
        onehot = (station_id == rec_v[:, i * per:(i + 1) * per]).astype(jnp.float32)
        sums = sums + jnp.dot(
            onehot.astype(jnp.bfloat16),
            window_v[i * per:(i + 1) * per, :],
            preferred_element_type=jnp.float32,
        )
    send_v[...] = (sums * taper_row).T

    chips = groups // CORES
    pl.semaphore_wait(barrier, (NOFF + 1) * chips)

    def band_copy(d, c, chip, number):
        return pltpu.make_async_remote_copy(
            src_ref=send_v.at[pl.ds((d + HALF) * BW, BW)],
            dst_ref=recv_v.at[TAKEN[c].index(d), off],
            send_sem=send_sem.at[number],
            recv_sem=recv_sem.at[TAKEN[c].index(d), off],
            device_id=(at_tile(d), chip * CORES + c),
            device_id_type=MESH,
        )

    def band_wait(slot, g):
        pltpu.make_async_remote_copy(
            src_ref=send_v.at[pl.ds(0, BW)],
            dst_ref=recv_v.at[slot, g],
            send_sem=send_sem.at[0],
            recv_sem=recv_sem.at[slot, g],
            device_id=(blk, sibling),
            device_id_type=MESH,
        ).wait_recv()

    outgoing = [
        (d, c, chip)
        for d in SEND_ORDER for c in range(CORES) if d in TAKEN[c] for chip in range(chips)
    ]

    def each_copy(act):
        for number, (d, c, chip) in enumerate(outgoing):
            copy = band_copy(d, c, chip, number)
            if d == 0:
                pl.when(off != chip * CORES + c)(functools.partial(act, copy))
            else:
                act(copy)

    each_copy(lambda copy: copy.start())

    home = TAKEN[1].index(0)

    @pl.when(core == 1)
    def _():
        recv_v[home, off] = send_v[HALF * BW:(HALF + 1) * BW, :]

    tabs_copy.wait()
    small[4].wait()
    cols = tab32.shape[0] // stations // 2
    slots = len(TAKEN[0])
    origins = [lax.rem(blk - taken(slot) + tiles, tiles) for slot in range(slots)]
    lane = lax.broadcasted_iota(jnp.int32, (1, tiles), 1)
    source_ids = [
        jnp.sum(jnp.where(lane == origin, src_v[...], 0), axis=1, keepdims=True)
        for origin in origins
    ]

    def widen(r, rows_of):
        span = pl.ds(pl.multiple_of(r * (2 * cols), 2 * cols), 2 * cols)
        wide = tabs_v[span, :].astype(jnp.float32)
        tab32[span, :] = wide
        return tuple(jnp.where(i == r, wide, old) for i, old in zip(source_ids, rows_of))

    blank = jnp.zeros((2 * cols, LANES), jnp.float32)
    found = lax.fori_loop(0, stations, widen, (blank,) * slots, unroll=4)
    for slot in range(slots):
        source_v[slot] = found[slot]

    def regroup(c, carry):
        for first_station in range(0, stations, STEP):
            row = first_station * 2 * cols + 2 * c
            time_v[c, first_station:first_station + STEP, :] = tab32[pl.ds(row, STEP, stride=2 * cols), :]
            amp_v[c, first_station:first_station + STEP, :] = tab32[pl.ds(row + 1, STEP, stride=2 * cols), :]
        return carry

    lax.fori_loop(0, cols, regroup, 0)

    def collect(pair):
        base = []
        slope = []
        for slot in pair:
            for g in range(groups):
                if slot == home:
                    @pl.when(jnp.logical_or(core == 0, off != g))
                    def _(g=g):
                        band_wait(slot, g)
                else:
                    band_wait(slot, g)
            total = (recv_v[slot, 0] + recv_v[slot, 1]) + (recv_v[slot, 2] + recv_v[slot, 3])
            after = jnp.concatenate([total[1:], total[BW - 1:]], axis=0)
            base.append(total)
            slope.append(after - total)
        rest = jnp.zeros((LANES - 4 * BW, stations), jnp.float32)
        both = jnp.concatenate(base + slope + [rest], axis=0).T
        for n, table in enumerate((both, pltpu.roll(both, LANES - 2 * BW, 1))):
            upper = table.astype(jnp.bfloat16)
            table_v[2 * n] = upper
            table_v[2 * n + 1] = (table - upper.astype(jnp.float32)).astype(jnp.bfloat16)

    def column(c, first_slot, count):
        acc = [jnp.zeros((STEP, LANES), jnp.float32) for _ in range(count)]
        time_at = [source_v[first_slot + n, pl.ds(2 * c, 1), :] for n in range(count)]
        amp_at = [source_v[first_slot + n, pl.ds(2 * c + 1, 1), :] for n in range(count)]
        for first_station in range(0, stations, STEP):
            span = slice(first_station, first_station + STEP)
            time = time_v[c, span, :]
            amp = amp_v[c, span, :]
            near = [table_v[n, span, :] for n in range(4)]
            for n in range(count):
                arrival = time_at[n] + time
                whole = arrival.astype(jnp.int32)
                part = arrival - whole.astype(jnp.float32)
                cell = whole.astype(jnp.int16)
                if n:
                    cell = cell + jnp.int16(BW)
                got = [lane_take(x, cell).astype(jnp.float32) for x in near]
                value = (got[0] + got[1]) + (got[2] + got[3]) * part
                acc[n] = acc[n] + amp * value
        whole_acc = amp_at[0] * acc[0]
        for n in range(1, count):
            whole_acc = whole_acc + amp_at[n] * acc[n]
        return jnp.sum(whole_acc, axis=0, keepdims=True)

    half = cols // CORES
    mine_first = core * half
    other_first = half - mine_first

    def early(c, carry):
        early_v[pl.ds(c, 1), :] = column(c, 0, 2)
        return carry

    def late(first, count):
        def step(i, carry):
            c = first + i
            out[core, pl.ds(c, 1), :] = (early_v[pl.ds(c, 1), :] + column(c, 2, count)) * scale
            return carry
        return step

    collect((0, 1))
    lax.fori_loop(0, cols, early, 0, unroll=2)
    collect((2, 3))
    lax.fori_loop(0, half, late(mine_first, 2), 0, unroll=2)
    lax.fori_loop(0, half, late(other_first, 1), 0, unroll=2)

    exchange = pltpu.make_async_remote_copy(
        src_ref=out.at[core],
        dst_ref=out.at[core],
        send_sem=peer_send_sem,
        recv_sem=peer_recv_sem,
        device_id=(blk, sibling),
        device_id_type=MESH,
    )
    exchange.start()
    pltpu.make_async_remote_copy(
        src_ref=out.at[core],
        dst_ref=out.at[1 - core],
        send_sem=peer_send_sem,
        recv_sem=peer_recv_sem,
        device_id=(blk, sibling),
        device_id_type=MESH,
    ).wait_recv()
    each_copy(lambda copy: copy.wait_send())
    exchange.wait_send()


def shards(traces, tables, band_start, src_vtation, rec_station, aperture, aperture_weight):
    tiles = lax.axis_size("blk")
    groups = lax.axis_size("off")
    rows, samples = traces.shape[2:]
    stations, _, points = tables.shape[1:]
    cols = points // LANES
    tabs = tables.reshape(stations, 2, cols, LANES).transpose(0, 2, 1, 3)
    tabs = tabs.reshape(stations * cols * 2, LANES)
    scale = 1.0 / math.sqrt(rows * groups * APER)
    any_spec = pl.BlockSpec(memory_space=pltpu.HBM)
    parts = pl.pallas_call(
        functools.partial(kernel, tiles, groups, scale),
        out_shape=pltpu.VMEM((CORES, cols, LANES), jnp.float32),
        in_specs=[any_spec] * 7,
        out_specs=pl.BlockSpec(memory_space=pltpu.VMEM),
        scratch_shapes=[
            pltpu.VMEM((rows, samples), jnp.bfloat16),
            pltpu.VMEM(tabs.shape, jnp.bfloat16),
            pltpu.VMEM(tabs.shape, jnp.float32),
            pltpu.VMEM((APER, 1, rows), jnp.int32),
            pltpu.VMEM((1, tiles), jnp.int32),
            pltpu.VMEM((1, rows), jnp.int32),
            pltpu.VMEM((APER, tiles), jnp.int32),
            pltpu.VMEM((APER, tiles), jnp.float32),
            pltpu.VMEM((rows, LANES), jnp.int16),
            pltpu.VMEM((rows, LANES), jnp.bfloat16),
            pltpu.VMEM((LANES, stations), jnp.float32),
            pltpu.VMEM((len(TAKEN[0]), groups, BW, stations), jnp.float32),
            pltpu.VMEM((4, stations, LANES), jnp.bfloat16),
            pltpu.VMEM((len(TAKEN[0]), 2 * cols, LANES), jnp.float32),
            pltpu.VMEM((cols, stations, LANES), jnp.float32),
            pltpu.VMEM((cols, stations, LANES), jnp.float32),
            pltpu.VMEM((cols, LANES), jnp.float32),
            pltpu.SemaphoreType.DMA((6,)),
            pltpu.SemaphoreType.DMA((CHUNKS,)),
            pltpu.SemaphoreType.DMA(((NOFF + 1) * groups // CORES,)),
            pltpu.SemaphoreType.DMA((len(TAKEN[0]), groups)),
            pltpu.SemaphoreType.DMA,
            pltpu.SemaphoreType.DMA,
        ],
        compiler_params=pltpu.CompilerParams(
            collective_id=0, has_side_effects=True, vmem_limit_bytes=60 * 1024 * 1024
        ),
        name="migrate",
    )(
        traces.reshape(rows, samples),
        tabs,
        band_start.reshape(APER, 1, rows),
        src_vtation.reshape(1, tiles),
        rec_station,
        aperture.T,
        aperture_weight.T,
    )
    return jnp.sum(parts, axis=0).reshape(1, points)


def solution(mesh):
    placed = (
        P("blk", "off", None, None),
        P("blk", None, None, None),
        P("blk", "off", None, None),
        P(),
        P(None, "off", None),
        P(),
        P(),
    )
    return jax.shard_map(
        shards, mesh=mesh, in_specs=placed, out_specs=P("blk", None), check_vma=False
    )
```

```python
import functools
import math

import jax
import jax.numpy as jnp
from jax import lax
from jax.experimental import pallas as pl
from jax.experimental.pallas import tpu as pltpu
from jax.sharding import PartitionSpec as P

BW = 16
APER = 5
HALF = 3
NOFF = 2 * HALF + 1
CORES = 2
SPLIT = 3
TAKEN = ((-2, -1, 1, SPLIT), (0, -3, 2, SPLIT))
SEND_ORDER = (3, 2, 1, 0, -1, -2, -3)
LANES = 128
CHUNKS = 4
STEP = 16
UNROLL = 16
MESH = pl.DeviceIdType.MESH


def lane_take(x, idx):
    numbers = lax.GatherDimensionNumbers(
        offset_dims=(),
        collapsed_slice_dims=(1,),
        start_index_map=(1,),
        operand_batching_dims=(0,),
        start_indices_batching_dims=(0,),
    )
    return lax.gather(
        x, idx[..., None], numbers, slice_sizes=(1, 1),
        mode=lax.GatherScatterMode.PROMISE_IN_BOUNDS,
    )


def kernel(
    tiles, groups, scale,
    traces, tabs, starts, src, rec, aper, aw,
    out,
    trace_v, tabs_v, tab32, starts_v, src_v, rec_v, aper_v, aw_v,
    pos_v, window_v, onehot_v, send_v, recv_v, table_v, source_v, time_v, amp_v, early_v,
    load_sem, chunk_sem, send_sem, recv_sem, peer_send_sem, peer_recv_sem, ready_sem,
):
    rows, samples = trace_v.shape
    stations = send_v.shape[1]
    blk = lax.axis_index("blk")
    off = lax.axis_index("off")

    def at_tile(d):
        return lax.rem(blk + (d + tiles), tiles)

    small = [
        pltpu.make_async_copy(starts, starts_v, load_sem.at[0]),
        pltpu.make_async_copy(aper, aper_v, load_sem.at[1]),
        pltpu.make_async_copy(rec.at[blk], rec_v, load_sem.at[2]),
        pltpu.make_async_copy(aw, aw_v, load_sem.at[3]),
        pltpu.make_async_copy(src, src_v, load_sem.at[4]),
    ]
    for copy in small:
        copy.start()
    per = rows // CHUNKS

    def chunk_copy(i):
        span = pl.ds(pl.multiple_of(i * per, per), per)
        return pltpu.make_async_copy(traces.at[span], trace_v.at[span], chunk_sem.at[i])

    for i in range(CHUNKS):
        chunk_copy(i).start()
    tabs_copy = pltpu.make_async_copy(tabs, tabs_v, load_sem.at[5])
    tabs_copy.start()

    core = lax.rem(off, CORES)
    chip_first = off - core
    sibling = chip_first + (1 - core)

    def taken(slot):
        return jnp.where(core == 0, TAKEN[0][slot], TAKEN[1][slot])

    barrier = pltpu.get_barrier_semaphore()

    def greet(tile, g):
        pl.semaphore_signal(barrier, inc=1, device_id=(tile, g), device_id_type=MESH)

    for c in range(CORES):
        @pl.when(core == c)
        def _(c=c):
            for d in reversed(TAKEN[c]):
                if d > 0:
                    for g in range(groups):
                        greet(at_tile(-d), g)
                elif d < 0:
                    @pl.when(blk - d < tiles)
                    def _(d=d):
                        for g in range(groups):
                            greet(at_tile(-d), g)
            if 0 in TAKEN[c]:
                for step in range(1, groups):
                    greet(blk, lax.rem(off + step, groups))
            else:
                greet(blk, sibling)

    chips = groups // CORES
    for c in range(CORES):
        for d in TAKEN[c]:
            if d < 0:
                @pl.when(blk + d < 0)
                def _(c=c, d=d):
                    for chip in range(chips):
                        greet(at_tile(d), chip * CORES + c)

    wraps_out = sum((blk + d < 0).astype(jnp.int32) for d in range(-HALF, 0))
    wraps_in = sum(
        jnp.logical_and(blk - d >= tiles, core == c).astype(jnp.int32)
        for c in range(CORES) for d in TAKEN[c] if d < 0
    )

    def enter():
        pl.semaphore_wait(barrier, (NOFF + 1) * chips - wraps_out * chips + wraps_in * groups)

    def answer():
        for c in range(CORES):
            for d in TAKEN[c]:
                if d < 0:
                    @pl.when(jnp.logical_and(blk - d >= tiles, core == c))
                    def _(d=d):
                        for g in range(groups):
                            pl.semaphore_signal(
                                ready_sem, inc=1, device_id=(at_tile(-d), g), device_id_type=MESH
                            )

    small[0].wait()
    small[1].wait()
    small[3].wait()
    mine = lax.broadcasted_iota(jnp.int32, (APER, tiles), 1) == blk
    target = jnp.sum(jnp.where(mine, aper_v[...], 0), axis=1, keepdims=True)
    taper = jnp.sum(jnp.where(mine, aw_v[...], 0.0), axis=1, keepdims=True)
    place = lax.rem(target - blk + (HALF + tiles), tiles)
    lane_off = lax.broadcasted_iota(jnp.int32, (APER, LANES), 1) // BW
    hit = (lane_off == place).astype(jnp.float32)
    taper_row = jnp.sum(hit * taper, axis=0, keepdims=True)
    begin = starts_v[:, 0, :]
    high = (begin >> 7).astype(jnp.float32)
    low = (begin & (LANES - 1)).astype(jnp.float32)
    fill = jnp.zeros((8 - APER, rows), jnp.float32)
    digits = jnp.concatenate([high, fill, low, fill], axis=0).astype(jnp.bfloat16)
    gap = jnp.zeros((8 - APER, LANES), jnp.float32)
    pick = jnp.concatenate([hit * LANES, gap, hit, gap], axis=0).astype(jnp.bfloat16)
    first = lax.dot_general(
        digits, pick, (((0,), (0,)), ((), ())), preferred_element_type=jnp.float32
    )
    tap = lax.broadcasted_iota(jnp.int32, (rows, LANES), 1) & (BW - 1)
    pos_v[...] = (first.astype(jnp.int32) + tap).astype(jnp.int16)

    small[2].wait()
    onehot = (
        lax.broadcasted_iota(jnp.int32, (stations, rows), 0) == rec_v[...]
    ).astype(jnp.float32).astype(jnp.bfloat16)
    onehot_v[...] = onehot
    for i in range(CHUNKS):
        chunk_copy(i).wait()
        if i == CHUNKS - 1:
            @pl.when(wraps_in > 0)
            def _():
                enter()
                answer()

        def do_rows(k, inner, i=i):
            span = pl.ds(pl.multiple_of(i * per + k * STEP, STEP), STEP)
            pos = pos_v[span, :]
            inside = pos & jnp.int16(LANES - 1)
            block = pos >> jnp.int16(7)
            acc = jnp.zeros((STEP, LANES), jnp.bfloat16)
            for c in range(samples // LANES):
                piece = lane_take(trace_v[span, c * LANES:(c + 1) * LANES], inside)
                acc = jnp.where(block == jnp.int16(c), piece, acc)
            window_v[span, :] = acc
            return inner

        lax.fori_loop(0, per // STEP, do_rows, 0, unroll=min(UNROLL, per // STEP))
    sums = jnp.dot(onehot_v[...], window_v[...], preferred_element_type=jnp.float32)
    send_v[...] = (sums * taper_row).T

    @pl.when(wraps_in == 0)
    def _():
        enter()

    def band_copy(d, c, chip, number):
        return pltpu.make_async_remote_copy(
            src_ref=send_v.at[pl.ds((d + HALF) * BW, BW)],
            dst_ref=recv_v.at[TAKEN[c].index(d), off],
            send_sem=send_sem.at[number],
            recv_sem=recv_sem.at[TAKEN[c].index(d), off],
            device_id=(at_tile(d), chip * CORES + c),
            device_id_type=MESH,
        )

    def band_wait(slot, g):
        pltpu.make_async_remote_copy(
            src_ref=send_v.at[pl.ds(0, BW)],
            dst_ref=recv_v.at[slot, g],
            send_sem=send_sem.at[0],
            recv_sem=recv_sem.at[slot, g],
            device_id=(blk, sibling),
            device_id_type=MESH,
        ).wait_recv()

    outgoing = [
        (d, c, chip)
        for d in SEND_ORDER for c in range(CORES) if d in TAKEN[c] for chip in range(chips)
    ]

    def each_copy(act):
        for number, (d, c, chip) in enumerate(outgoing):
            copy = band_copy(d, c, chip, number)
            if d == 0:
                pl.when(off != chip * CORES + c)(functools.partial(act, copy))
            else:
                act(copy)

    def start_straight():
        for number, (d, c, chip) in enumerate(outgoing):
            copy = band_copy(d, c, chip, number)
            if d < 0:
                pl.when(blk + d >= 0)(copy.start)
            elif d == 0:
                pl.when(off != chip * CORES + c)(copy.start)
            else:
                copy.start()

    def start_wrapped():
        @pl.when(wraps_out > 0)
        def _():
            pl.semaphore_wait(ready_sem, wraps_out * chips)
            for number, (d, c, chip) in enumerate(outgoing):
                if d < 0:
                    pl.when(blk + d < 0)(band_copy(d, c, chip, number).start)

    start_straight()
    home = TAKEN[1].index(0)

    @pl.when(core == 1)
    def _():
        recv_v[home, off] = send_v[HALF * BW:(HALF + 1) * BW, :]

    tabs_copy.wait()
    small[4].wait()
    cols = tab32.shape[0] // stations // 2
    slots = len(TAKEN[0])
    origins = [lax.rem(blk - taken(slot) + tiles, tiles) for slot in range(slots)]
    lane = lax.broadcasted_iota(jnp.int32, (1, tiles), 1)
    source_ids = [
        jnp.sum(jnp.where(lane == origin, src_v[...], 0), axis=1, keepdims=True)
        for origin in origins
    ]

    def widen(r, rows_of):
        span = pl.ds(pl.multiple_of(r * (2 * cols), 2 * cols), 2 * cols)
        wide = tabs_v[span, :].astype(jnp.float32)
        tab32[span, :] = wide
        return tuple(jnp.where(i == r, wide, old) for i, old in zip(source_ids, rows_of))

    blank = jnp.zeros((2 * cols, LANES), jnp.float32)
    found = lax.fori_loop(0, stations, widen, (blank,) * slots, unroll=4)
    for slot in range(slots):
        source_v[slot] = found[slot]

    def regroup(c, carry):
        for first_station in range(0, stations, STEP):
            row = first_station * 2 * cols + 2 * c
            time_v[c, first_station:first_station + STEP, :] = tab32[pl.ds(row, STEP, stride=2 * cols), :]
            amp_v[c, first_station:first_station + STEP, :] = tab32[pl.ds(row + 1, STEP, stride=2 * cols), :]
        return carry

    lax.fori_loop(0, cols, regroup, 0)

    def collect(pair):
        base = []
        slope = []
        for slot in pair:
            for g in range(groups):
                if slot == home:
                    @pl.when(jnp.logical_or(core == 0, off != g))
                    def _(g=g):
                        band_wait(slot, g)
                else:
                    band_wait(slot, g)
            total = (recv_v[slot, 0] + recv_v[slot, 1]) + (recv_v[slot, 2] + recv_v[slot, 3])
            after = jnp.concatenate([total[1:], total[BW - 1:]], axis=0)
            base.append(total)
            slope.append(after - total)
        rest = jnp.zeros((LANES - 4 * BW, stations), jnp.float32)
        both = jnp.concatenate(base + slope + [rest], axis=0).T
        for n, table in enumerate((both, pltpu.roll(both, LANES - 2 * BW, 1))):
            upper = table.astype(jnp.bfloat16)
            table_v[2 * n] = upper
            table_v[2 * n + 1] = (table - upper.astype(jnp.float32)).astype(jnp.bfloat16)

    def column(c, first_slot, count):
        acc = [jnp.zeros((STEP, LANES), jnp.float32) for _ in range(count)]
        time_at = [source_v[first_slot + n, pl.ds(2 * c, 1), :] for n in range(count)]
        amp_at = [source_v[first_slot + n, pl.ds(2 * c + 1, 1), :] for n in range(count)]
        for first_station in range(0, stations, STEP):
            span = slice(first_station, first_station + STEP)
            time = time_v[c, span, :]
            amp = amp_v[c, span, :]
            near = [table_v[n, span, :] for n in range(4)]
            for n in range(count):
                arrival = time_at[n] + time
                whole = arrival.astype(jnp.int32)
                part = arrival - whole.astype(jnp.float32)
                cell = whole.astype(jnp.int16)
                if n:
                    cell = cell + jnp.int16(BW)
                got = [lane_take(x, cell).astype(jnp.float32) for x in near]
                value = (got[0] + got[1]) + (got[2] + got[3]) * part
                acc[n] = acc[n] + amp * value
        whole_acc = amp_at[0] * acc[0]
        for n in range(1, count):
            whole_acc = whole_acc + amp_at[n] * acc[n]
        return jnp.sum(whole_acc, axis=0, keepdims=True)

    half = cols // CORES
    mine_first = core * half
    other_first = half - mine_first

    def early(c, carry):
        early_v[pl.ds(c, 1), :] = column(c, 0, 2)
        return carry

    def late(first, count):
        def step(i, carry):
            c = first + i
            out[core, pl.ds(c, 1), :] = (early_v[pl.ds(c, 1), :] + column(c, 2, count)) * scale
            return carry
        return step

    collect((0, 1))
    lax.fori_loop(0, cols, early, 0, unroll=2)
    start_wrapped()
    collect((2, 3))
    lax.fori_loop(0, half, late(mine_first, 2), 0, unroll=8)
    lax.fori_loop(0, half, late(other_first, 1), 0, unroll=8)

    exchange = pltpu.make_async_remote_copy(
        src_ref=out.at[core],
        dst_ref=out.at[core],
        send_sem=peer_send_sem,
        recv_sem=peer_recv_sem,
        device_id=(blk, sibling),
        device_id_type=MESH,
    )
    exchange.start()
    pltpu.make_async_remote_copy(
        src_ref=out.at[core],
        dst_ref=out.at[1 - core],
        send_sem=peer_send_sem,
        recv_sem=peer_recv_sem,
        device_id=(blk, sibling),
        device_id_type=MESH,
    ).wait_recv()
    each_copy(lambda copy: copy.wait_send())
    exchange.wait_send()


def shards(traces, tables, band_start, src_vtation, rec_station, aperture, aperture_weight):
    tiles = lax.axis_size("blk")
    groups = lax.axis_size("off")
    rows, samples = traces.shape[2:]
    stations, _, points = tables.shape[1:]
    cols = points // LANES
    tabs = tables.reshape(stations, 2, cols, LANES).transpose(0, 2, 1, 3)
    tabs = tabs.reshape(stations * cols * 2, LANES)
    scale = 1.0 / math.sqrt(rows * groups * APER)
    any_spec = pl.BlockSpec(memory_space=pltpu.HBM)
    parts = pl.pallas_call(
        functools.partial(kernel, tiles, groups, scale),
        out_shape=pltpu.VMEM((CORES, cols, LANES), jnp.float32),
        in_specs=[any_spec] * 7,
        out_specs=pl.BlockSpec(memory_space=pltpu.VMEM),
        scratch_shapes=[
            pltpu.VMEM((rows, samples), jnp.bfloat16),
            pltpu.VMEM(tabs.shape, jnp.bfloat16),
            pltpu.VMEM(tabs.shape, jnp.float32),
            pltpu.VMEM((APER, 1, rows), jnp.int32),
            pltpu.VMEM((1, tiles), jnp.int32),
            pltpu.VMEM((1, rows), jnp.int32),
            pltpu.VMEM((APER, tiles), jnp.int32),
            pltpu.VMEM((APER, tiles), jnp.float32),
            pltpu.VMEM((rows, LANES), jnp.int16),
            pltpu.VMEM((rows, LANES), jnp.bfloat16),
            pltpu.VMEM((stations, rows), jnp.bfloat16),
            pltpu.VMEM((LANES, stations), jnp.float32),
            pltpu.VMEM((len(TAKEN[0]), groups, BW, stations), jnp.float32),
            pltpu.VMEM((4, stations, LANES), jnp.bfloat16),
            pltpu.VMEM((len(TAKEN[0]), 2 * cols, LANES), jnp.float32),
            pltpu.VMEM((cols, stations, LANES), jnp.float32),
            pltpu.VMEM((cols, stations, LANES), jnp.float32),
            pltpu.VMEM((cols, LANES), jnp.float32),
            pltpu.SemaphoreType.DMA((6,)),
            pltpu.SemaphoreType.DMA((CHUNKS,)),
            pltpu.SemaphoreType.DMA(((NOFF + 1) * groups // CORES,)),
            pltpu.SemaphoreType.DMA((len(TAKEN[0]), groups)),
            pltpu.SemaphoreType.DMA,
            pltpu.SemaphoreType.DMA,
            pltpu.SemaphoreType.REGULAR,
        ],
        compiler_params=pltpu.CompilerParams(
            collective_id=0, has_side_effects=True, vmem_limit_bytes=60 * 1024 * 1024
        ),
        name="migrate",
    )(
        traces.reshape(rows, samples),
        tabs,
        band_start.reshape(APER, 1, rows),
        src_vtation.reshape(1, tiles),
        rec_station,
        aperture.T,
        aperture_weight.T,
    )
    return jnp.sum(parts, axis=0).reshape(1, points)


def solution(mesh):
    placed = (
        P("blk", "off", None, None),
        P("blk", None, None, None),
        P("blk", "off", None, None),
        P(),
        P(None, "off", None),
        P(),
        P(),
    )
    return jax.shard_map(
        shards, mesh=mesh, in_specs=placed, out_specs=P("blk", None), check_vma=False
    )
```

```python
import functools
import math

import jax
import jax.numpy as jnp
from jax import lax
from jax.experimental import pallas as pl
from jax.experimental.pallas import tpu as pltpu
from jax.sharding import PartitionSpec as P

BW = 16
APER = 5
HALF = 3
NOFF = 2 * HALF + 1
CORES = 2
SPLIT = 3
SHARE = 6
TAKEN = ((-2, -1, 1, SPLIT), (0, -3, 2, SPLIT))
SEND_ORDER = (3, 2, 1, 0, -1, -2, -3)
LANES = 128
CHUNKS = 4
STEP = 16
UNROLL = 16
MESH = pl.DeviceIdType.MESH


def lane_take(x, idx):
    numbers = lax.GatherDimensionNumbers(
        offset_dims=(),
        collapsed_slice_dims=(1,),
        start_index_map=(1,),
        operand_batching_dims=(0,),
        start_indices_batching_dims=(0,),
    )
    return lax.gather(
        x, idx[..., None], numbers, slice_sizes=(1, 1),
        mode=lax.GatherScatterMode.PROMISE_IN_BOUNDS,
    )


def kernel(
    tiles, groups, scale,
    traces, tabs, starts, src, rec, aper, aw,
    out,
    trace_v, tabs_v, tab32, starts_v, src_v, rec_v, aper_v, aw_v,
    pos_v, window_v, onehot_v, send_v, recv_v, table_v, source_v, time_v, amp_v, early_v,
    load_sem, chunk_sem, send_sem, recv_sem, peer_send_sem, peer_recv_sem, ready_sem,
):
    rows, samples = trace_v.shape
    stations = send_v.shape[1]
    blk = lax.axis_index("blk")
    off = lax.axis_index("off")

    def at_tile(d):
        return lax.rem(blk + (d + tiles), tiles)

    small = [
        pltpu.make_async_copy(starts, starts_v, load_sem.at[0]),
        pltpu.make_async_copy(aper, aper_v, load_sem.at[1]),
        pltpu.make_async_copy(rec.at[blk], rec_v, load_sem.at[2]),
        pltpu.make_async_copy(aw, aw_v, load_sem.at[3]),
        pltpu.make_async_copy(src, src_v, load_sem.at[4]),
    ]
    for copy in small:
        copy.start()
    per = rows // CHUNKS

    def chunk_copy(i):
        span = pl.ds(pl.multiple_of(i * per, per), per)
        return pltpu.make_async_copy(traces.at[span], trace_v.at[span], chunk_sem.at[i])

    for i in range(CHUNKS):
        chunk_copy(i).start()
    tabs_copy = pltpu.make_async_copy(tabs, tabs_v, load_sem.at[5])
    tabs_copy.start()

    core = lax.rem(off, CORES)
    chip_first = off - core
    sibling = chip_first + (1 - core)

    def taken(slot):
        return jnp.where(core == 0, TAKEN[0][slot], TAKEN[1][slot])

    barrier = pltpu.get_barrier_semaphore()

    def greet(tile, g):
        pl.semaphore_signal(barrier, inc=1, device_id=(tile, g), device_id_type=MESH)

    for c in range(CORES):
        @pl.when(core == c)
        def _(c=c):
            for d in reversed(TAKEN[c]):
                if d > 0:
                    for g in range(groups):
                        greet(at_tile(-d), g)
                elif d < 0:
                    @pl.when(blk - d < tiles)
                    def _(d=d):
                        for g in range(groups):
                            greet(at_tile(-d), g)
            if 0 in TAKEN[c]:
                for step in range(1, groups):
                    greet(blk, lax.rem(off + step, groups))
            else:
                greet(blk, sibling)

    chips = groups // CORES
    for c in range(CORES):
        for d in TAKEN[c]:
            if d < 0:
                @pl.when(blk + d < 0)
                def _(c=c, d=d):
                    for chip in range(chips):
                        greet(at_tile(d), chip * CORES + c)

    wraps_out = sum((blk + d < 0).astype(jnp.int32) for d in range(-HALF, 0))
    wraps_in = sum(
        jnp.logical_and(blk - d >= tiles, core == c).astype(jnp.int32)
        for c in range(CORES) for d in TAKEN[c] if d < 0
    )

    def enter():
        pl.semaphore_wait(barrier, (NOFF + 1) * chips - wraps_out * chips + wraps_in * groups)

    def answer():
        for c in range(CORES):
            for d in TAKEN[c]:
                if d < 0:
                    @pl.when(jnp.logical_and(blk - d >= tiles, core == c))
                    def _(d=d):
                        for g in range(groups):
                            pl.semaphore_signal(
                                ready_sem, inc=1, device_id=(at_tile(-d), g), device_id_type=MESH
                            )

    small[0].wait()
    small[1].wait()
    small[3].wait()
    mine = lax.broadcasted_iota(jnp.int32, (APER, tiles), 1) == blk
    target = jnp.sum(jnp.where(mine, aper_v[...], 0), axis=1, keepdims=True)
    taper = jnp.sum(jnp.where(mine, aw_v[...], 0.0), axis=1, keepdims=True)
    place = lax.rem(target - blk + (HALF + tiles), tiles)
    lane_off = lax.broadcasted_iota(jnp.int32, (APER, LANES), 1) // BW
    hit = (lane_off == place).astype(jnp.float32)
    taper_row = jnp.sum(hit * taper, axis=0, keepdims=True)
    begin = starts_v[:, 0, :]
    high = (begin >> 7).astype(jnp.float32)
    low = (begin & (LANES - 1)).astype(jnp.float32)
    fill = jnp.zeros((8 - APER, rows), jnp.float32)
    digits = jnp.concatenate([high, fill, low, fill], axis=0).astype(jnp.bfloat16)
    gap = jnp.zeros((8 - APER, LANES), jnp.float32)
    pick = jnp.concatenate([hit * LANES, gap, hit, gap], axis=0).astype(jnp.bfloat16)
    first = lax.dot_general(
        digits, pick, (((0,), (0,)), ((), ())), preferred_element_type=jnp.float32
    )
    tap = lax.broadcasted_iota(jnp.int32, (rows, LANES), 1) & (BW - 1)
    pos_v[...] = (first.astype(jnp.int32) + tap).astype(jnp.int16)

    small[2].wait()
    onehot = (
        lax.broadcasted_iota(jnp.int32, (stations, rows), 0) == rec_v[...]
    ).astype(jnp.float32).astype(jnp.bfloat16)
    onehot_v[...] = onehot
    for i in range(CHUNKS):
        chunk_copy(i).wait()
        if i == CHUNKS - 1:
            @pl.when(wraps_in > 0)
            def _():
                enter()
                answer()

        def do_rows(k, inner, i=i):
            span = pl.ds(pl.multiple_of(i * per + k * STEP, STEP), STEP)
            pos = pos_v[span, :]
            inside = pos & jnp.int16(LANES - 1)
            block = pos >> jnp.int16(7)
            acc = jnp.zeros((STEP, LANES), jnp.bfloat16)
            for c in range(samples // LANES):
                piece = lane_take(trace_v[span, c * LANES:(c + 1) * LANES], inside)
                acc = jnp.where(block == jnp.int16(c), piece, acc)
            window_v[span, :] = acc
            return inner

        lax.fori_loop(0, per // STEP, do_rows, 0, unroll=min(UNROLL, per // STEP))
    sums = jnp.dot(onehot_v[...], window_v[...], preferred_element_type=jnp.float32)
    send_v[...] = (sums * taper_row).T

    @pl.when(wraps_in == 0)
    def _():
        enter()

    def band_copy(d, c, chip, number):
        return pltpu.make_async_remote_copy(
            src_ref=send_v.at[pl.ds((d + HALF) * BW, BW)],
            dst_ref=recv_v.at[TAKEN[c].index(d), off],
            send_sem=send_sem.at[number],
            recv_sem=recv_sem.at[TAKEN[c].index(d), off],
            device_id=(at_tile(d), chip * CORES + c),
            device_id_type=MESH,
        )

    def band_wait(slot, g):
        pltpu.make_async_remote_copy(
            src_ref=send_v.at[pl.ds(0, BW)],
            dst_ref=recv_v.at[slot, g],
            send_sem=send_sem.at[0],
            recv_sem=recv_sem.at[slot, g],
            device_id=(blk, sibling),
            device_id_type=MESH,
        ).wait_recv()

    outgoing = [
        (d, c, chip)
        for d in SEND_ORDER for c in range(CORES) if d in TAKEN[c] for chip in range(chips)
    ]
    outgoing.sort(key=lambda entry: (entry[0] <= 0, entry[1]))

    def each_copy(act):
        for number, (d, c, chip) in enumerate(outgoing):
            copy = band_copy(d, c, chip, number)
            if d == 0:
                pl.when(off != chip * CORES + c)(functools.partial(act, copy))
            else:
                act(copy)

    def start_straight():
        for number, (d, c, chip) in enumerate(outgoing):
            copy = band_copy(d, c, chip, number)
            if d < 0:
                pl.when(blk + d >= 0)(copy.start)
            elif d == 0:
                pl.when(off != chip * CORES + c)(copy.start)
            else:
                copy.start()

    def start_wrapped():
        @pl.when(wraps_out > 0)
        def _():
            pl.semaphore_wait(ready_sem, wraps_out * chips)
            for number, (d, c, chip) in enumerate(outgoing):
                if d < 0:
                    pl.when(blk + d < 0)(band_copy(d, c, chip, number).start)

    start_straight()
    home = TAKEN[1].index(0)

    @pl.when(core == 1)
    def _():
        recv_v[home, off] = send_v[HALF * BW:(HALF + 1) * BW, :]

    tabs_copy.wait()
    small[4].wait()
    cols = tab32.shape[0] // stations // 2
    slots = len(TAKEN[0])
    origins = [lax.rem(blk - taken(slot) + tiles, tiles) for slot in range(slots)]
    lane = lax.broadcasted_iota(jnp.int32, (1, tiles), 1)
    source_ids = [
        jnp.sum(jnp.where(lane == origin, src_v[...], 0), axis=1, keepdims=True)
        for origin in origins
    ]

    def widen(r, rows_of):
        span = pl.ds(pl.multiple_of(r * (2 * cols), 2 * cols), 2 * cols)
        wide = tabs_v[span, :].astype(jnp.float32)
        tab32[span, :] = wide
        return tuple(jnp.where(i == r, wide, old) for i, old in zip(source_ids, rows_of))

    blank = jnp.zeros((2 * cols, LANES), jnp.float32)
    found = lax.fori_loop(0, stations, widen, (blank,) * slots, unroll=4)
    for slot in range(slots):
        source_v[slot] = found[slot]

    def regroup(c, carry):
        for first_station in range(0, stations, STEP):
            row = first_station * 2 * cols + 2 * c
            time_v[c, first_station:first_station + STEP, :] = tab32[pl.ds(row, STEP, stride=2 * cols), :]
            amp_v[c, first_station:first_station + STEP, :] = tab32[pl.ds(row + 1, STEP, stride=2 * cols), :]
        return carry

    lax.fori_loop(0, cols, regroup, 0)

    def collect(pair):
        base = []
        slope = []
        for slot in pair:
            for g in range(groups):
                if slot == home:
                    @pl.when(jnp.logical_or(core == 0, off != g))
                    def _(g=g):
                        band_wait(slot, g)
                else:
                    band_wait(slot, g)
            total = (recv_v[slot, 0] + recv_v[slot, 1]) + (recv_v[slot, 2] + recv_v[slot, 3])
            after = jnp.concatenate([total[1:], total[BW - 1:]], axis=0)
            base.append(total)
            slope.append(after - total)
        rest = jnp.zeros((LANES - 4 * BW, stations), jnp.float32)
        both = jnp.concatenate(base + slope + [rest], axis=0).T
        for n, table in enumerate((both, pltpu.roll(both, LANES - 2 * BW, 1))):
            upper = table.astype(jnp.bfloat16)
            table_v[2 * n] = upper
            table_v[2 * n + 1] = (table - upper.astype(jnp.float32)).astype(jnp.bfloat16)

    def column(c, first_slot, count):
        acc = [jnp.zeros((STEP, LANES), jnp.float32) for _ in range(count)]
        time_at = [source_v[first_slot + n, pl.ds(2 * c, 1), :] for n in range(count)]
        amp_at = [source_v[first_slot + n, pl.ds(2 * c + 1, 1), :] for n in range(count)]
        for first_station in range(0, stations, STEP):
            span = slice(first_station, first_station + STEP)
            time = time_v[c, span, :]
            amp = amp_v[c, span, :]
            near = [table_v[n, span, :] for n in range(4)]
            for n in range(count):
                arrival = time_at[n] + time
                whole = arrival.astype(jnp.int32)
                part = arrival - whole.astype(jnp.float32)
                cell = whole.astype(jnp.int16)
                if n:
                    cell = cell + jnp.int16(BW)
                got = [lane_take(x, cell).astype(jnp.float32) for x in near]
                value = (got[0] + got[1]) + (got[2] + got[3]) * part
                acc[n] = acc[n] + amp * value
        whole_acc = amp_at[0] * acc[0]
        for n in range(1, count):
            whole_acc = whole_acc + amp_at[n] * acc[n]
        return jnp.sum(whole_acc, axis=0, keepdims=True)

    def early(c, carry):
        early_v[pl.ds(c, 1), :] = column(c, 0, 2)
        return carry

    def late(first, count):
        def step(i, carry):
            c = first + i
            out[core, pl.ds(c, 1), :] = (early_v[pl.ds(c, 1), :] + column(c, 2, count)) * scale
            return carry
        return step

    collect((0, 1))
    lax.fori_loop(0, cols, early, 0, unroll=2)
    start_wrapped()
    collect((2, 3))
    for c in range(CORES):
        @pl.when(core == c)
        def _(c=c):
            whole = (0, SHARE) if c == 0 else (SHARE, cols)
            rest = (SHARE, cols) if c == 0 else (0, SHARE)
            for (first, last), count in ((whole, 2), (rest, 1)):
                lax.fori_loop(0, last - first, late(first, count), 0, unroll=last - first)

    exchange = pltpu.make_async_remote_copy(
        src_ref=out.at[core],
        dst_ref=out.at[core],
        send_sem=peer_send_sem,
        recv_sem=peer_recv_sem,
        device_id=(blk, sibling),
        device_id_type=MESH,
    )
    exchange.start()
    pltpu.make_async_remote_copy(
        src_ref=out.at[core],
        dst_ref=out.at[1 - core],
        send_sem=peer_send_sem,
        recv_sem=peer_recv_sem,
        device_id=(blk, sibling),
        device_id_type=MESH,
    ).wait_recv()
    each_copy(lambda copy: copy.wait_send())
    exchange.wait_send()


def shards(traces, tables, band_start, src_vtation, rec_station, aperture, aperture_weight):
    tiles = lax.axis_size("blk")
    groups = lax.axis_size("off")
    rows, samples = traces.shape[2:]
    stations, _, points = tables.shape[1:]
    cols = points // LANES
    tabs = tables.reshape(stations, 2, cols, LANES).transpose(0, 2, 1, 3)
    tabs = tabs.reshape(stations * cols * 2, LANES)
    scale = 1.0 / math.sqrt(rows * groups * APER)
    any_spec = pl.BlockSpec(memory_space=pltpu.HBM)
    parts = pl.pallas_call(
        functools.partial(kernel, tiles, groups, scale),
        out_shape=pltpu.VMEM((CORES, cols, LANES), jnp.float32),
        in_specs=[any_spec] * 7,
        out_specs=pl.BlockSpec(memory_space=pltpu.VMEM),
        scratch_shapes=[
            pltpu.VMEM((rows, samples), jnp.bfloat16),
            pltpu.VMEM(tabs.shape, jnp.bfloat16),
            pltpu.VMEM(tabs.shape, jnp.float32),
            pltpu.VMEM((APER, 1, rows), jnp.int32),
            pltpu.VMEM((1, tiles), jnp.int32),
            pltpu.VMEM((1, rows), jnp.int32),
            pltpu.VMEM((APER, tiles), jnp.int32),
            pltpu.VMEM((APER, tiles), jnp.float32),
            pltpu.VMEM((rows, LANES), jnp.int16),
            pltpu.VMEM((rows, LANES), jnp.bfloat16),
            pltpu.VMEM((stations, rows), jnp.bfloat16),
            pltpu.VMEM((LANES, stations), jnp.float32),
            pltpu.VMEM((len(TAKEN[0]), groups, BW, stations), jnp.float32),
            pltpu.VMEM((4, stations, LANES), jnp.bfloat16),
            pltpu.VMEM((len(TAKEN[0]), 2 * cols, LANES), jnp.float32),
            pltpu.VMEM((cols, stations, LANES), jnp.float32),
            pltpu.VMEM((cols, stations, LANES), jnp.float32),
            pltpu.VMEM((cols, LANES), jnp.float32),
            pltpu.SemaphoreType.DMA((6,)),
            pltpu.SemaphoreType.DMA((CHUNKS,)),
            pltpu.SemaphoreType.DMA(((NOFF + 1) * groups // CORES,)),
            pltpu.SemaphoreType.DMA((len(TAKEN[0]), groups)),
            pltpu.SemaphoreType.DMA,
            pltpu.SemaphoreType.DMA,
            pltpu.SemaphoreType.REGULAR,
        ],
        compiler_params=pltpu.CompilerParams(
            collective_id=0, has_side_effects=True, vmem_limit_bytes=60 * 1024 * 1024
        ),
        name="migrate",
    )(
        traces.reshape(rows, samples),
        tabs,
        band_start.reshape(APER, 1, rows),
        src_vtation.reshape(1, tiles),
        rec_station,
        aperture.T,
        aperture_weight.T,
    )
    return jnp.sum(parts, axis=0).reshape(1, points)


def solution(mesh):
    placed = (
        P("blk", "off", None, None),
        P("blk", None, None, None),
        P("blk", "off", None, None),
        P(),
        P(None, "off", None),
        P(),
        P(),
    )
    return jax.shard_map(
        shards, mesh=mesh, in_specs=placed, out_specs=P("blk", None), check_vma=False
    )
```

```python
import functools
import math

import jax
import jax.numpy as jnp
from jax import lax
from jax.experimental import pallas as pl
from jax.experimental.pallas import tpu as pltpu
from jax.sharding import PartitionSpec as P

BW = 16
APER = 5
HALF = 3
NOFF = 2 * HALF + 1
CORES = 2
SPLIT = 3
SHARE = 6
TAKEN = ((-2, -1, 1, SPLIT), (0, -3, 2, SPLIT))
SEND_ORDER = (3, 2, 1, 0, -1, -2, -3)
LANES = 128
CHUNKS = 4
STEP = 16
UNROLL = 16
MESH = pl.DeviceIdType.MESH


def lane_take(x, idx):
    numbers = lax.GatherDimensionNumbers(
        offset_dims=(),
        collapsed_slice_dims=(1,),
        start_index_map=(1,),
        operand_batching_dims=(0,),
        start_indices_batching_dims=(0,),
    )
    return lax.gather(
        x, idx[..., None], numbers, slice_sizes=(1, 1),
        mode=lax.GatherScatterMode.PROMISE_IN_BOUNDS,
    )


def kernel(
    tiles, groups, scale,
    traces, tabs, starts, src, rec, aper, aw,
    out,
    trace_v, tabs_v, tab32, starts_v, src_v, rec_v, aper_v, aw_v,
    pos_v, window_v, onehot_v, send_v, recv_v, table_v, flip_v, source_v, time_v, amp_v, early_v,
    load_sem, chunk_sem, send_sem, recv_sem, peer_send_sem, peer_recv_sem, ready_sem,
):
    rows, samples = trace_v.shape
    stations = send_v.shape[1]
    blk = lax.axis_index("blk")
    off = lax.axis_index("off")

    def at_tile(d):
        return lax.rem(blk + (d + tiles), tiles)

    small = [
        pltpu.make_async_copy(starts, starts_v, load_sem.at[0]),
        pltpu.make_async_copy(aper, aper_v, load_sem.at[1]),
        pltpu.make_async_copy(rec.at[blk], rec_v, load_sem.at[2]),
        pltpu.make_async_copy(aw, aw_v, load_sem.at[3]),
        pltpu.make_async_copy(src, src_v, load_sem.at[4]),
    ]
    small[0].start()
    small[1].start()
    per = rows // CHUNKS

    def chunk_copy(i):
        span = pl.ds(pl.multiple_of(i * per, per), per)
        return pltpu.make_async_copy(traces.at[span], trace_v.at[span], chunk_sem.at[i])

    chunk_copy(0).start()
    for copy in small[2:]:
        copy.start()
    for i in range(1, CHUNKS):
        chunk_copy(i).start()
    tabs_copy = pltpu.make_async_copy(tabs, tabs_v, load_sem.at[5])
    tabs_copy.start()

    core = lax.rem(off, CORES)
    chip_first = off - core
    sibling = chip_first + (1 - core)

    def taken(slot):
        return jnp.where(core == 0, TAKEN[0][slot], TAKEN[1][slot])

    barrier = pltpu.get_barrier_semaphore()

    def greet(tile, g):
        pl.semaphore_signal(barrier, inc=1, device_id=(tile, g), device_id_type=MESH)

    for c in range(CORES):
        @pl.when(core == c)
        def _(c=c):
            for d in reversed(TAKEN[c]):
                if d > 0:
                    for g in range(groups):
                        greet(at_tile(-d), g)
                elif d < 0:
                    @pl.when(blk - d < tiles)
                    def _(d=d):
                        for g in range(groups):
                            greet(at_tile(-d), g)
            if 0 in TAKEN[c]:
                for step in range(1, groups):
                    greet(blk, lax.rem(off + step, groups))
            else:
                greet(blk, sibling)

    chips = groups // CORES
    for c in range(CORES):
        for d in TAKEN[c]:
            if d < 0:
                @pl.when(blk + d < 0)
                def _(c=c, d=d):
                    for chip in range(chips):
                        greet(at_tile(d), chip * CORES + c)

    wraps_out = sum((blk + d < 0).astype(jnp.int32) for d in range(-HALF, 0))
    wraps_in = sum(
        jnp.logical_and(blk - d >= tiles, core == c).astype(jnp.int32)
        for c in range(CORES) for d in TAKEN[c] if d < 0
    )

    def enter():
        pl.semaphore_wait(barrier, (NOFF + 1) * chips - wraps_out * chips + wraps_in * groups)

    def answer():
        for c in range(CORES):
            for d in TAKEN[c]:
                if d < 0:
                    @pl.when(jnp.logical_and(blk - d >= tiles, core == c))
                    def _(d=d):
                        for g in range(groups):
                            pl.semaphore_signal(
                                ready_sem, inc=1, device_id=(at_tile(-d), g), device_id_type=MESH
                            )

    small[0].wait()
    small[1].wait()
    mine = lax.broadcasted_iota(jnp.int32, (APER, tiles), 1) == blk
    target = jnp.sum(jnp.where(mine, aper_v[...], 0), axis=1, keepdims=True)
    place = lax.rem(target - blk + (HALF + tiles), tiles)
    lane_off = lax.broadcasted_iota(jnp.int32, (APER, LANES), 1) // BW
    hit = (lane_off == place).astype(jnp.float32)
    begin = starts_v[:, 0, :]
    high = (begin >> 7).astype(jnp.float32)
    low = (begin & (LANES - 1)).astype(jnp.float32)
    fill = jnp.zeros((8 - APER, rows), jnp.float32)
    digits = jnp.concatenate([high, fill, low, fill], axis=0).astype(jnp.bfloat16)
    gap = jnp.zeros((8 - APER, LANES), jnp.float32)
    pick = jnp.concatenate([hit * LANES, gap, hit, gap], axis=0).astype(jnp.bfloat16)
    first = lax.dot_general(
        digits, pick, (((0,), (0,)), ((), ())), preferred_element_type=jnp.float32
    )
    tap = lax.broadcasted_iota(jnp.int32, (rows, LANES), 1) & (BW - 1)
    pos_v[...] = (first.astype(jnp.int32) + tap).astype(jnp.int16)

    small[2].wait()
    small[3].wait()
    taper = jnp.sum(jnp.where(mine, aw_v[...], 0.0), axis=1, keepdims=True)
    taper_row = jnp.sum(hit * taper, axis=0, keepdims=True)
    onehot = (
        lax.broadcasted_iota(jnp.int32, (stations, rows), 0) == rec_v[...]
    ).astype(jnp.float32).astype(jnp.bfloat16)
    onehot_v[...] = onehot
    for i in range(CHUNKS):
        chunk_copy(i).wait()
        if i == CHUNKS - 1:
            @pl.when(wraps_in > 0)
            def _():
                enter()
                answer()

        def do_rows(k, inner, i=i):
            span = pl.ds(pl.multiple_of(i * per + k * STEP, STEP), STEP)
            pos = pos_v[span, :]
            inside = pos & jnp.int16(LANES - 1)
            block = pos >> jnp.int16(7)
            acc = jnp.zeros((STEP, LANES), jnp.bfloat16)
            for c in range(samples // LANES):
                piece = lane_take(trace_v[span, c * LANES:(c + 1) * LANES], inside)
                acc = jnp.where(block == jnp.int16(c), piece, acc)
            window_v[span, :] = acc
            return inner

        lax.fori_loop(0, per // STEP, do_rows, 0, unroll=min(UNROLL, per // STEP))
    sums = jnp.dot(onehot_v[...], window_v[...], preferred_element_type=jnp.float32)
    send_v[...] = (sums * taper_row).T

    @pl.when(wraps_in == 0)
    def _():
        enter()

    def band_copy(d, c, chip, number):
        return pltpu.make_async_remote_copy(
            src_ref=send_v.at[pl.ds((d + HALF) * BW, BW)],
            dst_ref=recv_v.at[TAKEN[c].index(d), off],
            send_sem=send_sem.at[number],
            recv_sem=recv_sem.at[TAKEN[c].index(d), off],
            device_id=(at_tile(d), chip * CORES + c),
            device_id_type=MESH,
        )

    def band_wait(slot, g):
        pltpu.make_async_remote_copy(
            src_ref=send_v.at[pl.ds(0, BW)],
            dst_ref=recv_v.at[slot, g],
            send_sem=send_sem.at[0],
            recv_sem=recv_sem.at[slot, g],
            device_id=(blk, sibling),
            device_id_type=MESH,
        ).wait_recv()

    outgoing = [
        (d, c, chip)
        for d in SEND_ORDER for c in range(CORES) if d in TAKEN[c] for chip in range(chips)
    ]
    outgoing.sort(key=lambda entry: (entry[0] <= 0, entry[1]))

    def each_copy(act):
        for number, (d, c, chip) in enumerate(outgoing):
            copy = band_copy(d, c, chip, number)
            if d == 0:
                pl.when(off != chip * CORES + c)(functools.partial(act, copy))
            else:
                act(copy)

    def start_straight():
        for number, (d, c, chip) in enumerate(outgoing):
            copy = band_copy(d, c, chip, number)
            if d < 0:
                pl.when(blk + d >= 0)(copy.start)
            elif d == 0:
                pl.when(off != chip * CORES + c)(copy.start)
            else:
                copy.start()

    def start_wrapped():
        @pl.when(wraps_out > 0)
        def _():
            pl.semaphore_wait(ready_sem, wraps_out * chips)
            for number, (d, c, chip) in enumerate(outgoing):
                if d < 0:
                    pl.when(blk + d < 0)(band_copy(d, c, chip, number).start)

    start_straight()
    home = TAKEN[1].index(0)

    @pl.when(core == 1)
    def _():
        recv_v[home, off] = send_v[HALF * BW:(HALF + 1) * BW, :]

    flip_v[...] = jnp.zeros(flip_v.shape, jnp.float32)
    tabs_copy.wait()
    small[4].wait()
    cols = tabs_v.shape[0] // stations // 2
    slots = len(TAKEN[0])
    origins = [lax.rem(blk - taken(slot) + tiles, tiles) for slot in range(slots)]
    lane = lax.broadcasted_iota(jnp.int32, (1, tiles), 1)
    source_ids = [
        jnp.sum(jnp.where(lane == origin, src_v[...], 0), axis=1, keepdims=True)
        for origin in origins
    ]

    def widen(r, rows_of):
        span = pl.ds(pl.multiple_of(r * (2 * cols), 2 * cols), 2 * cols)
        wide = tabs_v[span, :].astype(jnp.float32)
        tab32[span, :] = wide
        return tuple(jnp.where(i == r, wide, old) for i, old in zip(source_ids, rows_of))

    blank = jnp.zeros((2 * cols, LANES), jnp.float32)
    found = lax.fori_loop(0, stations, widen, (blank,) * slots, unroll=4)
    for slot in range(slots):
        source_v[slot] = found[slot]

    def regroup(c, carry):
        for first_station in range(0, stations, STEP):
            row = first_station * 2 * cols + 2 * c
            time_v[c, first_station:first_station + STEP, :] = tab32[pl.ds(row, STEP, stride=2 * cols), :]
            amp_v[c, first_station:first_station + STEP, :] = tab32[pl.ds(row + 1, STEP, stride=2 * cols), :]
        return carry

    lax.fori_loop(0, cols, regroup, 0)

    def collect(pair):
        totals = []
        for slot in pair:
            for g in range(groups):
                if slot == home:
                    @pl.when(jnp.logical_or(core == 0, off != g))
                    def _(g=g):
                        band_wait(slot, g)
                else:
                    band_wait(slot, g)
            totals.append((recv_v[slot, 0] + recv_v[slot, 1]) + (recv_v[slot, 2] + recv_v[slot, 3]))
        flip_v[:, 0:2 * BW] = jnp.concatenate(totals, axis=0).T
        level = flip_v[...]
        step = pltpu.roll(level, LANES - 1, 1) - level
        for n, table in enumerate((level, step)):
            upper = table.astype(jnp.bfloat16)
            table_v[2 * n] = upper
            table_v[2 * n + 1] = (table - upper.astype(jnp.float32)).astype(jnp.bfloat16)

    def column(c, first_slot, count):
        acc = [jnp.zeros((STEP, LANES), jnp.float32) for _ in range(count)]
        time_at = [source_v[first_slot + n, pl.ds(2 * c, 1), :] for n in range(count)]
        amp_at = [source_v[first_slot + n, pl.ds(2 * c + 1, 1), :] for n in range(count)]
        for first_station in range(0, stations, STEP):
            span = slice(first_station, first_station + STEP)
            time = time_v[c, span, :]
            amp = amp_v[c, span, :]
            near = [table_v[n, span, :] for n in range(4)]
            for n in range(count):
                arrival = time_at[n] + time
                whole = arrival.astype(jnp.int32)
                part = arrival - whole.astype(jnp.float32)
                cell = whole.astype(jnp.int16)
                if n:
                    cell = cell + jnp.int16(BW)
                got = [lane_take(x, cell).astype(jnp.float32) for x in near]
                value = (got[0] + got[1]) + (got[2] + got[3]) * part
                acc[n] = acc[n] + amp * value
        whole_acc = amp_at[0] * acc[0]
        for n in range(1, count):
            whole_acc = whole_acc + amp_at[n] * acc[n]
        return jnp.sum(whole_acc, axis=0, keepdims=True)

    def early(c, carry):
        early_v[pl.ds(c, 1), :] = column(c, 0, 2)
        return carry

    def late(first, count):
        def step(i, carry):
            c = first + i
            out[core, pl.ds(c, 1), :] = (early_v[pl.ds(c, 1), :] + column(c, 2, count)) * scale
            return carry
        return step

    collect((0, 1))
    lax.fori_loop(0, cols, early, 0, unroll=4)
    start_wrapped()
    collect((2, 3))
    for c in range(CORES):
        @pl.when(core == c)
        def _(c=c):
            whole = (0, SHARE) if c == 0 else (SHARE, cols)
            rest = (SHARE, cols) if c == 0 else (0, SHARE)
            for (first, last), count in ((whole, 2), (rest, 1)):
                lax.fori_loop(0, last - first, late(first, count), 0, unroll=last - first)

    exchange = pltpu.make_async_remote_copy(
        src_ref=out.at[core],
        dst_ref=out.at[core],
        send_sem=peer_send_sem,
        recv_sem=peer_recv_sem,
        device_id=(blk, sibling),
        device_id_type=MESH,
    )
    exchange.start()
    pltpu.make_async_remote_copy(
        src_ref=out.at[core],
        dst_ref=out.at[1 - core],
        send_sem=peer_send_sem,
        recv_sem=peer_recv_sem,
        device_id=(blk, sibling),
        device_id_type=MESH,
    ).wait_recv()
    each_copy(lambda copy: copy.wait_send())
    exchange.wait_send()


def shards(traces, tables, band_start, src_vtation, rec_station, aperture, aperture_weight):
    tiles = lax.axis_size("blk")
    groups = lax.axis_size("off")
    rows, samples = traces.shape[2:]
    stations, _, points = tables.shape[1:]
    cols = points // LANES
    tabs = tables.reshape(stations, 2, cols, LANES).transpose(0, 2, 1, 3)
    tabs = tabs.reshape(stations * cols * 2, LANES)
    scale = 1.0 / math.sqrt(rows * groups * APER)
    any_spec = pl.BlockSpec(memory_space=pltpu.HBM)
    parts = pl.pallas_call(
        functools.partial(kernel, tiles, groups, scale),
        out_shape=pltpu.VMEM((CORES, cols, LANES), jnp.float32),
        in_specs=[any_spec] * 7,
        out_specs=pl.BlockSpec(memory_space=pltpu.VMEM),
        scratch_shapes=[
            pltpu.VMEM((rows, samples), jnp.bfloat16),
            pltpu.VMEM(tabs.shape, jnp.bfloat16),
            pltpu.VMEM((tabs.shape[0] + 2 * cols, LANES), jnp.float32),
            pltpu.VMEM((APER, 1, rows), jnp.int32),
            pltpu.VMEM((1, tiles), jnp.int32),
            pltpu.VMEM((1, rows), jnp.int32),
            pltpu.VMEM((APER, tiles), jnp.int32),
            pltpu.VMEM((APER, tiles), jnp.float32),
            pltpu.VMEM((rows, LANES), jnp.int16),
            pltpu.VMEM((rows, LANES), jnp.bfloat16),
            pltpu.VMEM((stations, rows), jnp.bfloat16),
            pltpu.VMEM((LANES, stations), jnp.float32),
            pltpu.VMEM((len(TAKEN[0]), groups, BW, stations), jnp.float32),
            pltpu.VMEM((4, stations, LANES), jnp.bfloat16),
            pltpu.VMEM((stations, LANES), jnp.float32),
            pltpu.VMEM((len(TAKEN[0]), 2 * cols, LANES), jnp.float32),
            pltpu.VMEM((cols, stations, LANES), jnp.float32),
            pltpu.VMEM((cols, stations, LANES), jnp.float32),
            pltpu.VMEM((cols, LANES), jnp.float32),
            pltpu.SemaphoreType.DMA((6,)),
            pltpu.SemaphoreType.DMA((CHUNKS,)),
            pltpu.SemaphoreType.DMA(((NOFF + 1) * groups // CORES,)),
            pltpu.SemaphoreType.DMA((len(TAKEN[0]), groups)),
            pltpu.SemaphoreType.DMA,
            pltpu.SemaphoreType.DMA,
            pltpu.SemaphoreType.REGULAR,
        ],
        compiler_params=pltpu.CompilerParams(
            collective_id=0, has_side_effects=True, vmem_limit_bytes=60 * 1024 * 1024
        ),
        name="migrate",
    )(
        traces.reshape(rows, samples),
        tabs,
        band_start.reshape(APER, 1, rows),
        src_vtation.reshape(1, tiles),
        rec_station,
        aperture.T,
        aperture_weight.T,
    )
    return jnp.sum(parts, axis=0).reshape(1, points)


def solution(mesh):
    placed = (
        P("blk", "off", None, None),
        P("blk", None, None, None),
        P("blk", "off", None, None),
        P(),
        P(None, "off", None),
        P(),
        P(),
    )
    return jax.shard_map(
        shards, mesh=mesh, in_specs=placed, out_specs=P("blk", None), check_vma=False
    )
```

```python
import functools
import math

import jax
import jax.numpy as jnp
from jax import lax
from jax.experimental import pallas as pl
from jax.experimental.pallas import tpu as pltpu
from jax.sharding import PartitionSpec as P

BW = 16
APER = 5
HALF = 3
NOFF = 2 * HALF + 1
CORES = 2
SPLIT = 3
SHARE = 6
TAKEN = ((-2, -1, 1, SPLIT), (0, -3, 2, SPLIT))
SEND_ORDER = (3, 2, 1, 0, -1, -2, -3)
LANES = 128
CHUNKS = 4
STEP = 16
UNROLL = 16
MESH = pl.DeviceIdType.MESH


def lane_take(x, idx):
    numbers = lax.GatherDimensionNumbers(
        offset_dims=(),
        collapsed_slice_dims=(1,),
        start_index_map=(1,),
        operand_batching_dims=(0,),
        start_indices_batching_dims=(0,),
    )
    return lax.gather(
        x, idx[..., None], numbers, slice_sizes=(1, 1),
        mode=lax.GatherScatterMode.PROMISE_IN_BOUNDS,
    )


def kernel(
    tiles, groups, scale,
    traces, tabs, starts, src, rec, aper, aw,
    out,
    trace_v, tabs_v, tab32, starts_v, src_v, rec_v, aper_v, aw_v,
    pos_v, window_v, onehot_v, send_v, recv_v, table_v, flip_v, source_v, time_v, amp_v, early_v,
    load_sem, chunk_sem, send_sem, recv_sem, peer_send_sem, peer_recv_sem, ready_sem,
):
    rows, samples = trace_v.shape
    stations = send_v.shape[1]
    blk = lax.axis_index("blk")
    off = lax.axis_index("off")

    def at_tile(d):
        return lax.rem(blk + (d + tiles), tiles)

    small = [
        pltpu.make_async_copy(starts, starts_v, load_sem.at[0]),
        pltpu.make_async_copy(aper, aper_v, load_sem.at[1]),
        pltpu.make_async_copy(rec.at[blk], rec_v, load_sem.at[2]),
        pltpu.make_async_copy(aw, aw_v, load_sem.at[3]),
        pltpu.make_async_copy(src, src_v, load_sem.at[4]),
    ]
    small[0].start()
    small[1].start()
    per = rows // CHUNKS

    def chunk_copy(i):
        span = pl.ds(pl.multiple_of(i * per, per), per)
        return pltpu.make_async_copy(traces.at[span], trace_v.at[span], chunk_sem.at[i])

    chunk_copy(0).start()
    for copy in small[2:]:
        copy.start()
    for i in range(1, CHUNKS):
        chunk_copy(i).start()
    tabs_copy = pltpu.make_async_copy(tabs, tabs_v, load_sem.at[5])
    tabs_copy.start()

    core = lax.rem(off, CORES)
    chip_first = off - core
    sibling = chip_first + (1 - core)

    def taken(slot):
        return jnp.where(core == 0, TAKEN[0][slot], TAKEN[1][slot])

    barrier = pltpu.get_barrier_semaphore()

    def greet(tile, g):
        pl.semaphore_signal(barrier, inc=1, device_id=(tile, g), device_id_type=MESH)

    for c in range(CORES):
        @pl.when(core == c)
        def _(c=c):
            for d in reversed(TAKEN[c]):
                if d > 0:
                    for g in range(groups):
                        greet(at_tile(-d), g)
                elif d < 0:
                    @pl.when(blk - d < tiles)
                    def _(d=d):
                        for g in range(groups):
                            greet(at_tile(-d), g)
            if 0 in TAKEN[c]:
                for step in range(1, groups):
                    greet(blk, lax.rem(off + step, groups))
            else:
                greet(blk, sibling)

    chips = groups // CORES
    for c in range(CORES):
        for d in TAKEN[c]:
            if d < 0:
                @pl.when(blk + d < 0)
                def _(c=c, d=d):
                    for chip in range(chips):
                        greet(at_tile(d), chip * CORES + c)

    wraps_out = sum((blk + d < 0).astype(jnp.int32) for d in range(-HALF, 0))
    wraps_in = sum(
        jnp.logical_and(blk - d >= tiles, core == c).astype(jnp.int32)
        for c in range(CORES) for d in TAKEN[c] if d < 0
    )

    def enter():
        pl.semaphore_wait(barrier, (NOFF + 1) * chips - wraps_out * chips + wraps_in * groups)

    def answer():
        for c in range(CORES):
            for d in TAKEN[c]:
                if d < 0:
                    @pl.when(jnp.logical_and(blk - d >= tiles, core == c))
                    def _(d=d):
                        for g in range(groups):
                            pl.semaphore_signal(
                                ready_sem, inc=1, device_id=(at_tile(-d), g), device_id_type=MESH
                            )

    small[0].wait()
    small[1].wait()
    mine = lax.broadcasted_iota(jnp.int32, (APER, tiles), 1) == blk
    target = jnp.sum(jnp.where(mine, aper_v[...], 0), axis=1, keepdims=True)
    place = lax.rem(target - blk + (HALF + tiles), tiles)
    lane_off = lax.broadcasted_iota(jnp.int32, (APER, LANES), 1) // BW
    hit = (lane_off == place).astype(jnp.float32)
    begin = starts_v[:, 0, :]
    high = (begin >> 7).astype(jnp.float32)
    low = (begin & (LANES - 1)).astype(jnp.float32)
    fill = jnp.zeros((8 - APER, rows), jnp.float32)
    digits = jnp.concatenate([high, fill, low, fill], axis=0).astype(jnp.bfloat16)
    gap = jnp.zeros((8 - APER, LANES), jnp.float32)
    pick = jnp.concatenate([hit * LANES, gap, hit, gap], axis=0).astype(jnp.bfloat16)
    first = lax.dot_general(
        digits, pick, (((0,), (0,)), ((), ())), preferred_element_type=jnp.float32
    )
    tap = lax.broadcasted_iota(jnp.int32, (rows, LANES), 1) & (BW - 1)
    pos_v[...] = (first.astype(jnp.int32) + tap).astype(jnp.int16)

    small[2].wait()
    onehot = (
        lax.broadcasted_iota(jnp.int32, (stations, rows), 0) == rec_v[...]
    ).astype(jnp.float32).astype(jnp.bfloat16)
    onehot_v[...] = onehot
    for i in range(CHUNKS):
        chunk_copy(i).wait()
        if i == CHUNKS - 1:
            @pl.when(wraps_in > 0)
            def _():
                enter()
                answer()

        def do_rows(k, inner, i=i):
            span = pl.ds(pl.multiple_of(i * per + k * STEP, STEP), STEP)
            pos = pos_v[span, :]
            inside = pos & jnp.int16(LANES - 1)
            block = pos >> jnp.int16(7)
            acc = jnp.zeros((STEP, LANES), jnp.bfloat16)
            for c in range(samples // LANES):
                piece = lane_take(trace_v[span, c * LANES:(c + 1) * LANES], inside)
                acc = jnp.where(block == jnp.int16(c), piece, acc)
            window_v[span, :] = acc
            return inner

        lax.fori_loop(0, per // STEP, do_rows, 0, unroll=min(UNROLL, per // STEP))
    small[3].wait()
    taper = jnp.sum(jnp.where(mine, aw_v[...], 0.0), axis=1, keepdims=True)
    taper_row = jnp.sum(hit * taper, axis=0, keepdims=True)
    sums = jnp.dot(onehot_v[...], window_v[...], preferred_element_type=jnp.float32)
    send_v[...] = (sums * taper_row).T

    @pl.when(wraps_in == 0)
    def _():
        enter()

    def band_copy(d, c, chip, number):
        return pltpu.make_async_remote_copy(
            src_ref=send_v.at[pl.ds((d + HALF) * BW, BW)],
            dst_ref=recv_v.at[TAKEN[c].index(d), off],
            send_sem=send_sem.at[number],
            recv_sem=recv_sem.at[TAKEN[c].index(d), off],
            device_id=(at_tile(d), chip * CORES + c),
            device_id_type=MESH,
        )

    def band_wait(slot, g):
        pltpu.make_async_remote_copy(
            src_ref=send_v.at[pl.ds(0, BW)],
            dst_ref=recv_v.at[slot, g],
            send_sem=send_sem.at[0],
            recv_sem=recv_sem.at[slot, g],
            device_id=(blk, sibling),
            device_id_type=MESH,
        ).wait_recv()

    outgoing = [
        (d, c, chip)
        for d in SEND_ORDER for c in range(CORES) if d in TAKEN[c] for chip in range(chips)
    ]
    outgoing.sort(key=lambda entry: (entry[0] <= 0, entry[1]))

    def each_copy(act):
        for number, (d, c, chip) in enumerate(outgoing):
            copy = band_copy(d, c, chip, number)
            if d == 0:
                pl.when(off != chip * CORES + c)(functools.partial(act, copy))
            else:
                act(copy)

    def start_straight():
        for number, (d, c, chip) in enumerate(outgoing):
            copy = band_copy(d, c, chip, number)
            if d < 0:
                pl.when(blk + d >= 0)(copy.start)
            elif d == 0:
                pl.when(off != chip * CORES + c)(copy.start)
            else:
                copy.start()

    def start_wrapped():
        @pl.when(wraps_out > 0)
        def _():
            pl.semaphore_wait(ready_sem, wraps_out * chips)
            for number, (d, c, chip) in enumerate(outgoing):
                if d < 0:
                    pl.when(blk + d < 0)(band_copy(d, c, chip, number).start)

    start_straight()
    home = TAKEN[1].index(0)

    @pl.when(core == 1)
    def _():
        recv_v[home, off] = send_v[HALF * BW:(HALF + 1) * BW, :]

    flip_v[...] = jnp.zeros(flip_v.shape, jnp.float32)
    tabs_copy.wait()
    small[4].wait()
    cols = tabs_v.shape[0] // stations // 2
    slots = len(TAKEN[0])
    origins = [lax.rem(blk - taken(slot) + tiles, tiles) for slot in range(slots)]
    lane = lax.broadcasted_iota(jnp.int32, (1, tiles), 1)
    source_ids = [
        jnp.sum(jnp.where(lane == origin, src_v[...], 0), axis=1, keepdims=True)
        for origin in origins
    ]

    def widen(r, rows_of):
        span = pl.ds(pl.multiple_of(r * (2 * cols), 2 * cols), 2 * cols)
        wide = tabs_v[span, :].astype(jnp.float32)
        tab32[span, :] = wide
        return tuple(jnp.where(i == r, wide, old) for i, old in zip(source_ids, rows_of))

    blank = jnp.zeros((2 * cols, LANES), jnp.float32)
    found = lax.fori_loop(0, stations, widen, (blank,) * slots, unroll=4)
    for slot in range(slots):
        source_v[slot] = found[slot]

    def regroup(c, carry):
        for first_station in range(0, stations, STEP):
            row = first_station * 2 * cols + 2 * c
            time_v[c, first_station:first_station + STEP, :] = tab32[pl.ds(row, STEP, stride=2 * cols), :]
            amp_v[c, first_station:first_station + STEP, :] = tab32[pl.ds(row + 1, STEP, stride=2 * cols), :]
        return carry

    lax.fori_loop(0, cols, regroup, 0)

    def collect(pair):
        totals = []
        for slot in pair:
            for g in range(groups):
                if slot == home:
                    @pl.when(jnp.logical_or(core == 0, off != g))
                    def _(g=g):
                        band_wait(slot, g)
                else:
                    band_wait(slot, g)
            totals.append((recv_v[slot, 0] + recv_v[slot, 1]) + (recv_v[slot, 2] + recv_v[slot, 3]))
        flip_v[:, 0:2 * BW] = jnp.concatenate(totals, axis=0).T
        level = flip_v[...]
        step = pltpu.roll(level, LANES - 1, 1) - level
        for n, table in enumerate((level, step)):
            upper = table.astype(jnp.bfloat16)
            table_v[2 * n] = upper
            table_v[2 * n + 1] = (table - upper.astype(jnp.float32)).astype(jnp.bfloat16)

    def column(c, first_slot, count):
        acc = [jnp.zeros((STEP, LANES), jnp.float32) for _ in range(count)]
        time_at = [source_v[first_slot + n, pl.ds(2 * c, 1), :] for n in range(count)]
        amp_at = [source_v[first_slot + n, pl.ds(2 * c + 1, 1), :] for n in range(count)]
        for first_station in range(0, stations, STEP):
            span = slice(first_station, first_station + STEP)
            time = time_v[c, span, :]
            amp = amp_v[c, span, :]
            near = [table_v[n, span, :] for n in range(4)]
            for n in range(count):
                arrival = time_at[n] + time
                whole = arrival.astype(jnp.int32)
                part = arrival - whole.astype(jnp.float32)
                cell = whole.astype(jnp.int16)
                if n:
                    cell = cell + jnp.int16(BW)
                got = [lane_take(x, cell).astype(jnp.float32) for x in near]
                value = (got[0] + got[1]) + (got[2] + got[3]) * part
                acc[n] = acc[n] + amp * value
        whole_acc = amp_at[0] * acc[0]
        for n in range(1, count):
            whole_acc = whole_acc + amp_at[n] * acc[n]
        return jnp.sum(whole_acc, axis=0, keepdims=True)

    def early(c, carry):
        early_v[pl.ds(c, 1), :] = column(c, 0, 2)
        return carry

    def late(first, count):
        def step(i, carry):
            c = first + i
            out[core, pl.ds(c, 1), :] = (early_v[pl.ds(c, 1), :] + column(c, 2, count)) * scale
            return carry
        return step

    collect((0, 1))
    lax.fori_loop(0, cols, early, 0, unroll=8)
    start_wrapped()
    collect((2, 3))
    for c in range(CORES):
        @pl.when(core == c)
        def _(c=c):
            whole = (0, SHARE) if c == 0 else (SHARE, cols)
            rest = (SHARE, cols) if c == 0 else (0, SHARE)
            for (first, last), count in ((whole, 2), (rest, 1)):
                lax.fori_loop(0, last - first, late(first, count), 0, unroll=last - first)

    exchange = pltpu.make_async_remote_copy(
        src_ref=out.at[core],
        dst_ref=out.at[core],
        send_sem=peer_send_sem,
        recv_sem=peer_recv_sem,
        device_id=(blk, sibling),
        device_id_type=MESH,
    )
    exchange.start()
    pltpu.make_async_remote_copy(
        src_ref=out.at[core],
        dst_ref=out.at[1 - core],
        send_sem=peer_send_sem,
        recv_sem=peer_recv_sem,
        device_id=(blk, sibling),
        device_id_type=MESH,
    ).wait_recv()
    each_copy(lambda copy: copy.wait_send())
    exchange.wait_send()


def shards(traces, tables, band_start, src_vtation, rec_station, aperture, aperture_weight):
    tiles = lax.axis_size("blk")
    groups = lax.axis_size("off")
    rows, samples = traces.shape[2:]
    stations, _, points = tables.shape[1:]
    cols = points // LANES
    tabs = tables.reshape(stations, 2, cols, LANES).transpose(0, 2, 1, 3)
    tabs = tabs.reshape(stations * cols * 2, LANES)
    scale = 1.0 / math.sqrt(rows * groups * APER)
    any_spec = pl.BlockSpec(memory_space=pltpu.HBM)
    parts = pl.pallas_call(
        functools.partial(kernel, tiles, groups, scale),
        out_shape=pltpu.VMEM((CORES, cols, LANES), jnp.float32),
        in_specs=[any_spec] * 7,
        out_specs=pl.BlockSpec(memory_space=pltpu.VMEM),
        scratch_shapes=[
            pltpu.VMEM((rows, samples), jnp.bfloat16),
            pltpu.VMEM(tabs.shape, jnp.bfloat16),
            pltpu.VMEM((tabs.shape[0] + 2 * cols, LANES), jnp.float32),
            pltpu.VMEM((APER, 1, rows), jnp.int32),
            pltpu.VMEM((1, tiles), jnp.int32),
            pltpu.VMEM((1, rows), jnp.int32),
            pltpu.VMEM((APER, tiles), jnp.int32),
            pltpu.VMEM((APER, tiles), jnp.float32),
            pltpu.VMEM((rows, LANES), jnp.int16),
            pltpu.VMEM((rows, LANES), jnp.bfloat16),
            pltpu.VMEM((stations, rows), jnp.bfloat16),
            pltpu.VMEM((LANES, stations), jnp.float32),
            pltpu.VMEM((len(TAKEN[0]), groups, BW, stations), jnp.float32),
            pltpu.VMEM((4, stations, LANES), jnp.bfloat16),
            pltpu.VMEM((stations, LANES), jnp.float32),
            pltpu.VMEM((len(TAKEN[0]), 2 * cols, LANES), jnp.float32),
            pltpu.VMEM((cols, stations, LANES), jnp.float32),
            pltpu.VMEM((cols, stations, LANES), jnp.float32),
            pltpu.VMEM((cols, LANES), jnp.float32),
            pltpu.SemaphoreType.DMA((6,)),
            pltpu.SemaphoreType.DMA((CHUNKS,)),
            pltpu.SemaphoreType.DMA(((NOFF + 1) * groups // CORES,)),
            pltpu.SemaphoreType.DMA((len(TAKEN[0]), groups)),
            pltpu.SemaphoreType.DMA,
            pltpu.SemaphoreType.DMA,
            pltpu.SemaphoreType.REGULAR,
        ],
        compiler_params=pltpu.CompilerParams(
            collective_id=0, has_side_effects=True, vmem_limit_bytes=60 * 1024 * 1024
        ),
        name="migrate",
    )(
        traces.reshape(rows, samples),
        tabs,
        band_start.reshape(APER, 1, rows),
        src_vtation.reshape(1, tiles),
        rec_station,
        aperture.T,
        aperture_weight.T,
    )
    return jnp.sum(parts, axis=0).reshape(1, points)


def solution(mesh):
    placed = (
        P("blk", "off", None, None),
        P("blk", None, None, None),
        P("blk", "off", None, None),
        P(),
        P(None, "off", None),
        P(),
        P(),
    )
    return jax.shard_map(
        shards, mesh=mesh, in_specs=placed, out_specs=P("blk", None), check_vma=False
    )
```
